32 devices in a mesh: groups: 2 (over x), ctx: 16 (over z, y, core).
Axes of the slice: x: 2, y: 2, z: 4, core: 2. Of those that a mesh axis runs over, the one named last changes fastest.
Arguments:
- queries: bfloat16 [128, 4096], P(('groups', 'ctx')), parts along dimension 0, may hold values from -110 to 110
- keys: bfloat16 [16, 65536, 128], P(None, ('groups', 'ctx')), parts along dimension 1, may hold values from -8 to 8
- values: bfloat16 [16, 65536, 128], P(None, ('groups', 'ctx')), parts along dimension 1, may hold values from -6 to 6
- residual: bfloat16 [128, 5376], P(('groups', 'ctx')), parts along dimension 0, may hold values from -6 to 6
- post_gain: float32 [5376], replicated, may hold values from 0.5 to 1.5
- out_weight: bfloat16 [4096, 5376], P('ctx'), may hold values from -0.09375 to 0.09375
Outputs:
- updated: float32 [128, 5376], P(('groups', 'ctx')), parts along dimension 0
The draws below stay inside these ranges and needn't reach their ends.
There are 2 independent parts, one for each index of `groups`. The reference program is written for one: setup_inputs(seed, part) draws one part's arguments, and reference() takes and returns one part's arrays. A program takes and returns all parts, laid end to end along the dimension named above; an argument that names none is the same for every part. Nothing has to cross between parts.
All inputs are finite; a program needn't handle non-finite values.
Results may differ from the reference program's by a relative error of at most 0.017.
Values may be sent and summed in bfloat16 or wider, within the bound.
A program may use at most 320 MiB of HBM per device.

```python
import jax
import jax.numpy as jnp
from jax import lax

D = 5376
HEADS = 32
KV_HEADS = 16
HEAD_DIM = 128
UNITS = 64
CONTEXT = 32768
N_CTX = 16


def plant_table(key):
    plant_key = jax.random.fold_in(key, 101)
    signs = jnp.where(jax.random.bernoulli(jax.random.fold_in(plant_key, 1), 0.5, (8, HEAD_DIM)), 1.0, -1.0)
    sizes = jax.random.uniform(jax.random.fold_in(plant_key, 3), (8, HEAD_DIM), jnp.float32, 1.0, 1.5)
    vectors = signs * sizes
    places = jax.random.randint(jax.random.fold_in(plant_key, 2), (8,), 0, CONTEXT // 2) * 2
    target = 120.0 + 40.0 * jnp.arange(8, dtype=jnp.float32)
    key_vectors = 5.0 * vectors
    length_sq = jnp.sum(vectors * key_vectors, axis=1)
    factor = target * jnp.sqrt(168.0) / length_sq
    heads_hit = (2 * jnp.arange(8) + 1) % HEADS
    units_hit = jnp.arange(8) * (UNITS // 8)
    return (vectors, key_vectors, places, target, factor, heads_hit, units_hit)


def draw_keys(key, part):
    base = jnp.clip(jax.random.normal(jax.random.fold_in(key, 11), (KV_HEADS, CONTEXT, HEAD_DIM), jnp.float32), -4.0, 4.0)
    vectors, key_vectors, places, target, factor, heads_hit, units_hit = plant_table(key)
    kv_hit = heads_hit // (HEADS // KV_HEADS)
    base = base.at[kv_hit, places].set(key_vectors)
    base = base.at[kv_hit, places + 1].set(key_vectors * (1.0 - 2.0 / target)[:, None])
    return base.astype(jnp.bfloat16)


def draw_queries(key, part):
    base = jnp.clip(jax.random.normal(jax.random.fold_in(key, 21), (UNITS, HEADS, HEAD_DIM), jnp.float32), -4.0, 4.0)
    vectors, key_vectors, places, target, factor, heads_hit, units_hit = plant_table(key)
    base = base.at[units_hit, heads_hit].set(factor[:, None] * vectors)
    return base.reshape(UNITS, HEADS * HEAD_DIM).astype(jnp.bfloat16)


def steps_of(rng, extent, shards, smallest, largest):
    gain = 1.0
    for dim, parts in shards:
        heights = jax.random.uniform(jax.random.fold_in(jax.random.fold_in(rng, 6), dim), (parts,), jnp.float32, smallest / len(shards), largest / len(shards))
        gain = gain * jnp.repeat(jnp.exp(heights), extent[dim] // parts).reshape((-1,) + (1,) * (len(extent) - 1 - dim))
    return gain


def centred(rng, shape, width, reach, cuts=(), kind=jnp.bfloat16):
    factor_of = steps_of(rng, shape, cuts, -0.22, 0.18) if cuts else 1.0
    entries = jax.random.normal(rng, shape, jnp.float32) * width * factor_of
    return jnp.minimum(jnp.maximum(entries, -reach), reach).astype(kind)


def setup_inputs(seed: int = 0, part: int = 0) -> dict:
    splits = jax.random.split(jax.random.key(seed), 7)
    part_splits = jax.random.split(jax.random.fold_in(splits[6], part), 7)
    return {
        "queries": draw_queries(jax.random.fold_in(jax.random.fold_in(splits[6], part), 71), part),
        "keys": draw_keys(jax.random.fold_in(jax.random.fold_in(splits[6], part), 71), part),
        "values": centred(part_splits[2], (KV_HEADS, CONTEXT, HEAD_DIM), 1.0, 6.0, ((1, 16),)),
        "residual": centred(part_splits[3], (UNITS, D), 1.0, 6.0, ((0, 16),)),
        "post_gain": jnp.clip(1.0 + 0.1 * jax.random.normal(splits[4], (D,), jnp.float32), 0.5, 1.5),
        "out_weight": centred(splits[5], (HEADS * HEAD_DIM, D), (HEADS * HEAD_DIM) ** -0.5, 0.09375, ((0, 16),)),
    }


query_scale = 168.0 ** (-0.5)

def attend_head(operands):
    head_queries, head_keys, head_values = operands
    scores = lax.dot_general(head_queries, head_keys, (((1,), (1,)), ((), ())), preferred_element_type=jnp.float32) * query_scale
    row_max = lax.optimization_barrier(jnp.max(scores, axis=1, keepdims=True))
    exponent = jnp.exp(scores - row_max)
    row_total = lax.optimization_barrier(jnp.sum(exponent, axis=1, keepdims=True))
    weights = exponent.astype(jnp.bfloat16)
    weighted = jnp.dot(weights, head_values, preferred_element_type=jnp.float32)
    return (weighted / row_total).astype(jnp.bfloat16)

def reference(queries, keys, values, residual, post_gain, out_weight):
    unit_count = queries.shape[0]
    group_size = HEADS // KV_HEADS
    grouped = queries.reshape(unit_count, KV_HEADS, group_size, HEAD_DIM).transpose(1, 0, 2, 3).reshape(KV_HEADS, unit_count * group_size, HEAD_DIM)
    attended = lax.map(attend_head, (grouped, keys, values))
    attended = attended.reshape(KV_HEADS, unit_count, group_size, HEAD_DIM).transpose(1, 0, 2, 3).reshape(unit_count, HEADS * HEAD_DIM)
    shard_width = HEADS * HEAD_DIM // N_CTX
    pieces = attended.reshape(unit_count, N_CTX, shard_width).transpose(1, 0, 2)
    weight_pieces = out_weight.reshape(N_CTX, shard_width, D)

    def accumulate(carry, operands):
        piece, weight_piece = operands
        term = jnp.dot(piece, weight_piece, preferred_element_type=jnp.float32).astype(jnp.bfloat16)
        term = lax.optimization_barrier(term)
        return (carry + term.astype(jnp.float32), None)
    branch, _ = lax.scan(accumulate, jnp.zeros((unit_count, D), jnp.float32), (pieces, weight_pieces))
    mean_square = lax.optimization_barrier(jnp.mean(branch * branch, axis=1, keepdims=True))
    normed = branch * lax.rsqrt(mean_square + 1e-06) * post_gain
    return residual.astype(jnp.float32) + normed
```

```python
import functools
import math

import jax
import jax.numpy as jnp
from jax import lax
from jax.experimental import pallas as pl
from jax.experimental.pallas import tpu as pltpu
from jax.sharding import PartitionSpec as P

MESH = pl.DeviceIdType.MESH
f32, bf16 = jnp.float32, jnp.bfloat16


def chunk_of(extent, largest):
    return max(c for c in range(128, largest + 1, 128) if extent % c == 0)


def kernel(
    n,
    group_size,
    q_ref,
    k_hbm,
    v_hbm,
    res_ref,
    gain_ref,
    w_hbm,
    out_ref,
    k_buf,
    v_buf,
    w_buf,
    q_all,
    part_out,
    stat_out,
    part_in,
    stat_in,
    y_out,
    y_in,
    k_sem,
    v_sem,
    w_sem,
    q_send,
    q_recv,
    p_send,
    p_recv,
    s_send,
    s_recv,
    y_send,
    y_recv,
):
    me = lax.axis_index("ctx")
    core = lax.rem(me, 2)
    sibling = me + 1 - 2 * core
    kv_heads, context, head_dim = k_buf.shape
    own_units = q_ref.shape[0]
    owners = n // kv_heads
    own_heads = group_size // owners
    own_rows = own_units * group_size
    rows = n * own_rows
    units = n * own_units
    width = w_buf.shape[1]
    scale = 168.0**-0.5 * math.log2(math.e)
    own_head = lax.div(me, owners)

    def head_at(step):
        return lax.rem(own_head + 1 + step, kv_heads)

    def k_copy(h):
        return pltpu.make_async_copy(k_hbm.at[h], k_buf.at[h], k_sem.at[h])

    def v_copy(h):
        return pltpu.make_async_copy(v_hbm.at[h], v_buf.at[h], v_sem.at[h])

    w_copy = pltpu.make_async_copy(w_hbm, w_buf, w_sem)

    @pl.loop(0, kv_heads)
    def _(step):
        k_copy(head_at(step)).start()
        v_copy(head_at(step)).start()

    w_copy.start()

    barrier = pltpu.get_barrier_semaphore()

    @pl.loop(1, n)
    def _(step):
        pl.semaphore_signal(
            barrier, inc=1, device_id={"ctx": lax.rem(me + step, n)}, device_id_type=MESH
        )

    own = q_ref[...].astype(f32)
    for h in range(kv_heads):
        first = h * group_size * head_dim
        q_all[me, h] = jnp.concatenate(
            [own[:, first + g * head_dim :][:, :head_dim] for g in range(group_size)], axis=0
        ).astype(bf16)

    pl.semaphore_wait(barrier, n - 1)

    def q_copy(block, target, slot):
        return pltpu.make_async_remote_copy(
            src_ref=q_all.at[block],
            dst_ref=q_all.at[block],
            send_sem=q_send.at[slot],
            recv_sem=q_recv.at[block],
            device_id={"ctx": target},
            device_id_type=MESH,
        )

    half = n // 2

    def peer(step):
        return lax.rem(me + 2 * step, n)

    @pl.loop(1, half)
    def _(step):
        q_copy(me, peer(step), step).start()

    q_copy(me, sibling, 0).start()

    @pl.loop(1, half)
    def _(step):
        source = peer(half - step)
        q_copy(source, sibling, 0).wait_recv()
        q_copy(source, sibling, half + step).start()

    @pl.loop(0, half)
    def _(step):
        q_copy(lax.rem(sibling + 2 * step, n), sibling, 0).wait_recv()

    def part_copy(h, p, source):
        slot = h * owners + p
        return (
            pltpu.make_async_remote_copy(
                src_ref=part_out.at[h],
                dst_ref=part_in.at[source],
                send_sem=p_send.at[slot],
                recv_sem=p_recv.at[source],
                device_id={"ctx": slot},
                device_id_type=MESH,
            ),
            pltpu.make_async_remote_copy(
                src_ref=stat_out.at[h],
                dst_ref=stat_in.at[source],
                send_sem=s_send.at[slot],
                recv_sem=s_recv.at[source],
                device_id={"ctx": slot},
                device_id_type=MESH,
            ),
        )

    tile = chunk_of(context, 512)

    @pl.loop(0, kv_heads)
    def _(step):
        h = head_at(step)
        q = q_all[:, h].astype(f32).reshape(rows, head_dim).astype(bf16)
        k_copy(h).wait()
        scores = [
            lax.dot_general(
                k_buf[h, pl.ds(t, tile), :],
                q,
                (((1,), (1,)), ((), ())),
                preferred_element_type=f32,
            )
            for t in range(0, context, tile)
        ]
        peak = functools.reduce(
            jnp.maximum, [jnp.max(s, axis=0, keepdims=True) for s in scores]
        ) * scale
        v_copy(h).wait()
        total = jnp.zeros((1, rows), f32)
        weighted = jnp.zeros((head_dim, rows), f32)
        for i, s in enumerate(scores):
            exponent = jnp.exp2(s * scale - peak)
            total += jnp.sum(exponent, axis=0, keepdims=True)
            weighted += lax.dot_general(
                v_buf[h, pl.ds(i * tile, tile), :],
                exponent.astype(bf16),
                (((0,), (0,)), ((), ())),
                preferred_element_type=f32,
            )
        row = lax.broadcasted_iota(jnp.int32, (8, rows), 0)
        part_out[h] = weighted.astype(bf16)
        stat_out[h] = jnp.where(row == 0, peak, total)
        for p in range(owners):

            @pl.when(h * owners + p != me)
            def _():
                for copy in part_copy(h, p, me):
                    copy.start()

    part_in[me] = part_out[own_head]
    stat_in[me] = stat_out[own_head]

    @pl.loop(1, n)
    def _(step):
        for copy in part_copy(0, 0, lax.rem(me + step, n)):
            copy.wait_recv()

    stats = stat_in[...]
    overall = jnp.max(stats, axis=0)[0:1, :]
    total = jnp.zeros((1, rows), f32)
    weighted = jnp.zeros((head_dim, rows), f32)
    for k in range(n):
        factor = jnp.exp2(stats[k, 0:1, :] - overall)
        total += factor * stats[k, 1:2, :]
        weighted += factor * part_in[k].astype(f32)
    attended = (weighted / total).astype(bf16)

    unit = lax.broadcasted_iota(jnp.int32, (units, rows), 0)
    column = lax.broadcasted_iota(jnp.int32, (units, rows), 1)
    first = lax.rem(me, owners) * own_heads
    blocks = []
    for g in range(own_heads):
        place = (
            lax.div(unit, own_units) * own_rows + (first + g) * own_units + lax.rem(unit, own_units)
        )
        pick = jnp.where(column == place, 1.0, 0.0).astype(bf16)
        blocks.append(
            lax.dot_general(
                pick, attended, (((1,), (1,)), ((), ())), preferred_element_type=f32
            ).astype(bf16)
        )
    own_block = jnp.concatenate(blocks, axis=1) if own_heads > 1 else blocks[0]

    w_copy.wait()
    step_width = chunk_of(width, 1024)
    for c in range(0, width, step_width):
        y = jnp.dot(own_block, w_buf[:, c : c + step_width], preferred_element_type=f32)
        for k in range(n):
            y_out[k, :, c : c + step_width] = y[k * own_units : (k + 1) * own_units].astype(bf16)

    def y_copy(target, source):
        return pltpu.make_async_remote_copy(
            src_ref=y_out.at[target],
            dst_ref=y_in.at[source],
            send_sem=y_send.at[target],
            recv_sem=y_recv.at[source],
            device_id={"ctx": target},
            device_id_type=MESH,
        )

    @pl.loop(1, n)
    def _(step):
        y_copy(lax.rem(me + step, n), me).start()

    y_in[me] = y_out[me]

    @pl.loop(1, n)
    def _(step):
        y_copy(me, lax.rem(me + step, n)).wait_recv()

    branch = jnp.zeros((own_units, width), f32)
    for k in range(n):
        branch += y_in[k].astype(f32)
    mean_square = jnp.mean(branch * branch, axis=1, keepdims=True)
    normed = branch * lax.rsqrt(mean_square + 1e-06) * gain_ref[...]
    out_ref[...] = res_ref[...].astype(f32) + normed

    @pl.loop(1, half)
    def _(step):
        q_copy(me, sibling, step).wait_send()
        q_copy(me, sibling, half + step).wait_send()

    q_copy(me, sibling, 0).wait_send()

    @pl.loop(1, n)
    def _(step):
        target = lax.rem(me + step, n)
        for copy in part_copy(lax.div(target, owners), lax.rem(target, owners), me):
            copy.wait_send()
        y_copy(target, me).wait_send()


def shards(n, queries, keys, values, residual, post_gain, out_weight):
    kv_heads, context, head_dim = keys.shape
    own_units, all_width = queries.shape
    head_count = all_width // head_dim
    group_size = head_count // kv_heads
    own_rows = own_units * group_size
    rows = n * own_rows
    width = residual.shape[1]
    vmem = pl.BlockSpec(memory_space=pltpu.VMEM)
    hbm = pl.BlockSpec(memory_space=pl.ANY)
    dma = pltpu.SemaphoreType.DMA
    return pl.pallas_call(
        functools.partial(kernel, n, group_size),
        out_shape=jax.ShapeDtypeStruct((own_units, width), f32),
        in_specs=[vmem, hbm, hbm, vmem, vmem, hbm],
        out_specs=vmem,
        scratch_shapes=[
            pltpu.VMEM(keys.shape, bf16),
            pltpu.VMEM(values.shape, bf16),
            pltpu.VMEM(out_weight.shape, bf16),
            pltpu.VMEM((n, kv_heads, own_rows, head_dim), bf16),
            pltpu.VMEM((kv_heads, head_dim, rows), bf16),
            pltpu.VMEM((kv_heads, 8, rows), f32),
            pltpu.VMEM((n, head_dim, rows), bf16),
            pltpu.VMEM((n, 8, rows), f32),
            pltpu.VMEM((n, own_units, width), bf16),
            pltpu.VMEM((n, own_units, width), bf16),
            dma((kv_heads,)),
            dma((kv_heads,)),
            dma,
            dma((n,)),
            dma((n,)),
            dma((n,)),
            dma((n,)),
            dma((n,)),
            dma((n,)),
            dma((n,)),
            dma((n,)),
        ],
        compiler_params=pltpu.CompilerParams(
            collective_id=0, has_side_effects=True, vmem_limit_bytes=56 * 2**20
        ),
        cost_estimate=pl.CostEstimate(
            flops=4 * kv_heads * context * rows * head_dim,
            bytes_accessed=4 * kv_heads * context * head_dim,
            transcendentals=kv_heads * context * rows,
        ),
    )(queries, keys, values, residual, post_gain.reshape(1, width), out_weight)


def solution(mesh):
    in_specs = (
        P(("groups", "ctx"), None),
        P(None, ("groups", "ctx"), None),
        P(None, ("groups", "ctx"), None),
        P(("groups", "ctx"), None),
        P(),
        P("ctx", None),
    )
    out_specs = P(("groups", "ctx"), None)
    return jax.shard_map(
        functools.partial(shards, mesh.shape["ctx"]),
        mesh=mesh,
        in_specs=in_specs,
        out_specs=out_specs,
        check_vma=False,
    )
```

```python
import functools
import math

import jax
import jax.numpy as jnp
from jax import lax
from jax.experimental import pallas as pl
from jax.experimental.pallas import tpu as pltpu
from jax.sharding import PartitionSpec as P

MESH = pl.DeviceIdType.MESH
f32, bf16 = jnp.float32, jnp.bfloat16


def chunk_of(extent, largest):
    return max(c for c in range(128, largest + 1, 128) if extent % c == 0)


def kernel(
    n,
    group_size,
    q_ref,
    k_hbm,
    v_hbm,
    res_ref,
    gain_ref,
    w_hbm,
    out_ref,
    k_buf,
    v_buf,
    w_buf,
    q_all,
    part_out,
    stat_out,
    part_in,
    stat_in,
    y_out,
    core_in,
    across_out,
    across_in,
    z_out,
    z_in,
    k_sem,
    v_sem,
    w_sem,
    q_send,
    q_recv,
    p_send,
    p_recv,
    s_send,
    s_recv,
    y_send,
    y_recv,
    z_send,
    z_recv,
):
    me = lax.axis_index("ctx")
    core = lax.rem(me, 2)
    sibling = me + 1 - 2 * core
    depth = n // 4
    y = lax.rem(lax.div(me, 2), 2)
    z = lax.div(me, 4)

    def device(its_z, its_y, its_core):
        return (its_z * 2 + its_y) * 2 + its_core

    across = device(z, 1 - y, core)
    kv_heads, context, head_dim = k_buf.shape
    own_units = q_ref.shape[0]
    owners = n // kv_heads
    own_heads = group_size // owners
    own_rows = own_units * group_size
    rows = n * own_rows
    units = n * own_units
    width = w_buf.shape[1]
    scale = 168.0**-0.5 * math.log2(math.e)
    own_head = lax.div(me, owners)

    def head_at(step):
        return lax.rem(own_head + 1 + step, kv_heads)

    def k_copy(h):
        return pltpu.make_async_copy(k_hbm.at[h], k_buf.at[h], k_sem.at[h])

    def v_copy(h):
        return pltpu.make_async_copy(v_hbm.at[h], v_buf.at[h], v_sem.at[h])

    w_copy = pltpu.make_async_copy(w_hbm, w_buf, w_sem)

    @pl.loop(0, kv_heads)
    def _(step):
        k_copy(head_at(step)).start()
        v_copy(head_at(step)).start()

    w_copy.start()

    barrier = pltpu.get_barrier_semaphore()

    @pl.loop(1, n)
    def _(step):
        pl.semaphore_signal(
            barrier, inc=1, device_id={"ctx": lax.rem(me + step, n)}, device_id_type=MESH
        )

    own = q_ref[...].astype(f32)
    for h in range(kv_heads):
        first = h * group_size * head_dim
        q_all[me, h] = jnp.concatenate(
            [own[:, first + g * head_dim :][:, :head_dim] for g in range(group_size)], axis=0
        ).astype(bf16)

    pl.semaphore_wait(barrier, n - 1)

    def q_copy(block, target, slot):
        return pltpu.make_async_remote_copy(
            src_ref=q_all.at[block],
            dst_ref=q_all.at[block],
            send_sem=q_send.at[slot],
            recv_sem=q_recv.at[block],
            device_id={"ctx": target},
            device_id_type=MESH,
        )

    def at_z(step, its_y):
        return device(lax.rem(z + step, depth), its_y, core)

    @pl.loop(1, depth)
    def _(step):
        q_copy(me, at_z(step, y), step).start()

    q_copy(me, across, 0).start()
    q_copy(me, sibling, depth).start()

    @pl.loop(1, depth)
    def _(step):
        source = at_z(depth - step, y)
        q_copy(source, sibling, 0).wait_recv()
        q_copy(source, across, 2 * depth + step).start()
        q_copy(source, sibling, depth + step).start()

    @pl.loop(0, depth)
    def _(step):
        source = at_z(depth - step, 1 - y)
        q_copy(source, sibling, 0).wait_recv()
        q_copy(source, sibling, 3 * depth + step).start()

    @pl.loop(0, n // 2)
    def _(step):
        q_copy(2 * step + 1 - core, sibling, 0).wait_recv()

    def part_copy(h, p, source):
        slot = h * owners + p
        return (
            pltpu.make_async_remote_copy(
                src_ref=part_out.at[h],
                dst_ref=part_in.at[source],
                send_sem=p_send.at[slot],
                recv_sem=p_recv.at[source],
                device_id={"ctx": slot},
                device_id_type=MESH,
            ),
            pltpu.make_async_remote_copy(
                src_ref=stat_out.at[h],
                dst_ref=stat_in.at[source],
                send_sem=s_send.at[slot],
                recv_sem=s_recv.at[source],
                device_id={"ctx": slot},
                device_id_type=MESH,
            ),
        )

    tile = chunk_of(context, 512)

    @pl.loop(0, kv_heads)
    def _(step):
        h = head_at(step)
        q = q_all[:, h].astype(f32).reshape(rows, head_dim).astype(bf16)
        k_copy(h).wait()
        scores = [
            lax.dot_general(
                k_buf[h, pl.ds(t, tile), :],
                q,
                (((1,), (1,)), ((), ())),
                preferred_element_type=f32,
            )
            for t in range(0, context, tile)
        ]
        peak = functools.reduce(
            jnp.maximum, [jnp.max(s, axis=0, keepdims=True) for s in scores]
        ) * scale
        v_copy(h).wait()
        total = jnp.zeros((1, rows), f32)
        weighted = jnp.zeros((head_dim, rows), f32)
        for i, s in enumerate(scores):
            exponent = jnp.exp2(s * scale - peak)
            total += jnp.sum(exponent, axis=0, keepdims=True)
            weighted += lax.dot_general(
                v_buf[h, pl.ds(i * tile, tile), :],
                exponent.astype(bf16),
                (((0,), (0,)), ((), ())),
                preferred_element_type=f32,
            )
        row = lax.broadcasted_iota(jnp.int32, (8, rows), 0)
        part_out[h] = weighted.astype(bf16)
        stat_out[h] = jnp.where(row == 0, peak, total)
        for p in range(owners):

            @pl.when(h * owners + p != me)
            def _():
                for copy in part_copy(h, p, me):
                    copy.start()

    part_in[me] = part_out[own_head]
    stat_in[me] = stat_out[own_head]

    @pl.loop(1, n)
    def _(step):
        for copy in part_copy(0, 0, lax.rem(me + step, n)):
            copy.wait_recv()

    stats = stat_in[...]
    overall = jnp.max(stats, axis=0)[0:1, :]
    total = jnp.zeros((1, rows), f32)
    weighted = jnp.zeros((head_dim, rows), f32)
    for k in range(n):
        factor = jnp.exp2(stats[k, 0:1, :] - overall)
        total += factor * stats[k, 1:2, :]
        weighted += factor * part_in[k].astype(f32)
    attended = (weighted / total).astype(bf16)

    unit = lax.broadcasted_iota(jnp.int32, (units, rows), 0)
    column = lax.broadcasted_iota(jnp.int32, (units, rows), 1)
    first = lax.rem(me, owners) * own_heads
    blocks = []
    for g in range(own_heads):
        place = (
            lax.div(unit, own_units) * own_rows + (first + g) * own_units + lax.rem(unit, own_units)
        )
        pick = jnp.where(column == place, 1.0, 0.0).astype(bf16)
        blocks.append(
            lax.dot_general(
                pick, attended, (((1,), (1,)), ((), ())), preferred_element_type=f32
            ).astype(bf16)
        )
    own_block = jnp.concatenate(blocks, axis=1) if own_heads > 1 else blocks[0]

    w_copy.wait()

    def core_copy(c):
        return pltpu.make_async_remote_copy(
            src_ref=y_out.at[c, 1 - core],
            dst_ref=core_in.at[c],
            send_sem=y_send.at[0, c],
            recv_sem=y_recv.at[0, c],
            device_id={"ctx": sibling},
            device_id_type=MESH,
        )

    def across_copy(c):
        return pltpu.make_async_remote_copy(
            src_ref=across_out.at[c],
            dst_ref=across_in.at[c],
            send_sem=y_send.at[1, c],
            recv_sem=y_recv.at[1, c],
            device_id={"ctx": across},
            device_id_type=MESH,
        )

    def z_copy(c, target, source):
        return pltpu.make_async_remote_copy(
            src_ref=z_out.at[c, target],
            dst_ref=z_in.at[c, source],
            send_sem=z_send.at[c, target],
            recv_sem=z_recv.at[c, source],
            device_id={"ctx": device(target, y, core)},
            device_id_type=MESH,
        )

    chunks = y_out.shape[0]
    cols = y_out.shape[-1]
    for c in range(chunks):
        product = jnp.dot(
            own_block, w_buf[:, c * cols : (c + 1) * cols], preferred_element_type=f32
        )
        for k in range(n):
            y_out[c, k % 2, k // 2 % 2, k // 4] = product[
                k * own_units : (k + 1) * own_units
            ].astype(bf16)
        core_copy(c).start()
    for c in range(chunks):
        core_copy(c).wait_recv()
        across_out[c] = (
            y_out[c, core, 1 - y].astype(f32) + core_in[c, 1 - y].astype(f32)
        ).astype(bf16)
        across_copy(c).start()
    for c in range(chunks):
        own_sum = y_out[c, core, y].astype(f32) + core_in[c, y].astype(f32)
        across_copy(c).wait_recv()
        z_out[c] = (own_sum + across_in[c].astype(f32)).astype(bf16)

        @pl.loop(1, depth)
        def _(step):
            z_copy(c, lax.rem(z + step, depth), z).start()

        z_in[c, z] = z_out[c, z]
    branches = []
    for c in range(chunks):

        @pl.loop(1, depth)
        def _(step):
            z_copy(c, z, lax.rem(z + step, depth)).wait_recv()

        branches.append(jnp.sum(z_in[c].astype(f32), axis=0))
    squares = sum(jnp.sum(b * b, axis=1, keepdims=True) for b in branches)
    inverse = lax.rsqrt(squares / width + 1e-06)
    for c, branch in enumerate(branches):
        at = pl.ds(c * cols, cols)
        gain = gain_ref[at].reshape(1, cols)
        out_ref[:, at] = res_ref[:, at].astype(f32) + branch * inverse * gain

    @pl.loop(0, n)
    def _(step):
        @pl.when(step != 2 * depth)
        def _():
            q_copy(me, sibling, step).wait_send()

    @pl.loop(1, n)
    def _(step):
        target = lax.rem(me + step, n)
        for copy in part_copy(lax.div(target, owners), lax.rem(target, owners), me):
            copy.wait_send()

    for c in range(chunks):
        core_copy(c).wait_send()
        across_copy(c).wait_send()

        @pl.loop(1, depth)
        def _(step):
            z_copy(c, lax.rem(z + step, depth), z).wait_send()


def shards(n, queries, keys, values, residual, post_gain, out_weight):
    kv_heads, context, head_dim = keys.shape
    own_units, all_width = queries.shape
    head_count = all_width // head_dim
    group_size = head_count // kv_heads
    own_rows = own_units * group_size
    rows = n * own_rows
    width = residual.shape[1]
    cols = chunk_of(width, 2048)
    chunks = width // cols
    depth = n // 4
    vmem = pl.BlockSpec(memory_space=pltpu.VMEM)
    hbm = pl.BlockSpec(memory_space=pl.ANY)
    dma = pltpu.SemaphoreType.DMA
    return pl.pallas_call(
        functools.partial(kernel, n, group_size),
        out_shape=jax.ShapeDtypeStruct((own_units, width), f32),
        in_specs=[vmem, hbm, hbm, vmem, vmem, hbm],
        out_specs=vmem,
        scratch_shapes=[
            pltpu.VMEM(keys.shape, bf16),
            pltpu.VMEM(values.shape, bf16),
            pltpu.VMEM(out_weight.shape, bf16),
            pltpu.VMEM((n, kv_heads, own_rows, head_dim), bf16),
            pltpu.VMEM((kv_heads, head_dim, rows), bf16),
            pltpu.VMEM((kv_heads, 8, rows), f32),
            pltpu.VMEM((n, head_dim, rows), bf16),
            pltpu.VMEM((n, 8, rows), f32),
            pltpu.VMEM((chunks, 2, 2, depth, own_units, cols), bf16),
            pltpu.VMEM((chunks, 2, depth, own_units, cols), bf16),
            pltpu.VMEM((chunks, depth, own_units, cols), bf16),
            pltpu.VMEM((chunks, depth, own_units, cols), bf16),
            pltpu.VMEM((chunks, depth, own_units, cols), bf16),
            pltpu.VMEM((chunks, depth, own_units, cols), bf16),
            dma((kv_heads,)),
            dma((kv_heads,)),
            dma,
            dma((n,)),
            dma((n,)),
            dma((n,)),
            dma((n,)),
            dma((n,)),
            dma((n,)),
            dma((2, chunks)),
            dma((2, chunks)),
            dma((chunks, depth)),
            dma((chunks, depth)),
        ],
        compiler_params=pltpu.CompilerParams(
            collective_id=0, has_side_effects=True, vmem_limit_bytes=56 * 2**20
        ),
        cost_estimate=pl.CostEstimate(
            flops=4 * kv_heads * context * rows * head_dim,
            bytes_accessed=4 * kv_heads * context * head_dim,
            transcendentals=kv_heads * context * rows,
        ),
    )(queries, keys, values, residual, post_gain, out_weight)


def solution(mesh):
    in_specs = (
        P(("groups", "ctx"), None),
        P(None, ("groups", "ctx"), None),
        P(None, ("groups", "ctx"), None),
        P(("groups", "ctx"), None),
        P(),
        P("ctx", None),
    )
    out_specs = P(("groups", "ctx"), None)
    return jax.shard_map(
        functools.partial(shards, mesh.shape["ctx"]),
        mesh=mesh,
        in_specs=in_specs,
        out_specs=out_specs,
        check_vma=False,
    )
```

```python
import functools
import math

import jax
import jax.numpy as jnp
from jax import lax
from jax.experimental import pallas as pl
from jax.experimental.pallas import tpu as pltpu
from jax.sharding import PartitionSpec as P

MESH = pl.DeviceIdType.MESH
f32, bf16 = jnp.float32, jnp.bfloat16


def chunk_of(extent, largest):
    return max(c for c in range(128, largest + 1, 128) if extent % c == 0)


def kernel(
    n,
    group_size,
    q_ref,
    k_hbm,
    v_hbm,
    res_ref,
    gain_ref,
    w_hbm,
    out_ref,
    k_buf,
    v_buf,
    w_buf,
    q_all,
    part_out,
    stat_out,
    part_in,
    stat_in,
    y_out,
    core_in,
    across_out,
    across_in,
    z_out,
    z_in,
    k_sem,
    v_sem,
    w_sem,
    q_send,
    q_recv,
    p_send,
    p_recv,
    s_send,
    s_recv,
    y_send,
    y_recv,
    z_send,
    z_recv,
):
    me = lax.axis_index("ctx")
    core = lax.rem(me, 2)
    sibling = me + 1 - 2 * core
    depth = n // 4
    y = lax.rem(lax.div(me, 2), 2)
    z = lax.div(me, 4)

    def device(its_z, its_y, its_core):
        return (its_z * 2 + its_y) * 2 + its_core

    across = device(z, 1 - y, core)
    kv_heads, context, head_dim = k_buf.shape
    own_units = q_ref.shape[0]
    owners = n // kv_heads
    own_heads = group_size // owners
    own_rows = own_units * group_size
    rows = n * own_rows
    units = n * own_units
    width = w_buf.shape[1]
    scale = 168.0**-0.5 * math.log2(math.e)
    own_head = lax.div(me, owners)

    def head_at(step):
        return lax.rem(own_head + 1 + step, kv_heads)

    def k_copy(h):
        return pltpu.make_async_copy(k_hbm.at[h], k_buf.at[h], k_sem.at[h])

    def v_copy(h):
        return pltpu.make_async_copy(v_hbm.at[h], v_buf.at[h], v_sem.at[h])

    w_copy = pltpu.make_async_copy(w_hbm, w_buf, w_sem)

    @pl.loop(0, kv_heads)
    def _(step):
        k_copy(head_at(step)).start()
        v_copy(head_at(step)).start()

    w_copy.start()

    barrier = pltpu.get_barrier_semaphore()

    @pl.loop(1, n)
    def _(step):
        pl.semaphore_signal(
            barrier, inc=1, device_id={"ctx": lax.rem(me + step, n)}, device_id_type=MESH
        )

    own = q_ref[...].astype(f32)
    for h in range(kv_heads):
        first = h * group_size * head_dim
        q_all[me, h] = jnp.concatenate(
            [own[:, first + g * head_dim :][:, :head_dim] for g in range(group_size)], axis=0
        ).astype(bf16)

    pl.semaphore_wait(barrier, n - 1)

    def q_copy(block, target, slot):
        return pltpu.make_async_remote_copy(
            src_ref=q_all.at[block],
            dst_ref=q_all.at[block],
            send_sem=q_send.at[slot],
            recv_sem=q_recv.at[block],
            device_id={"ctx": target},
            device_id_type=MESH,
        )

    def at_z(step, its_y):
        return device(lax.rem(z + step, depth), its_y, core)

    @pl.loop(1, depth)
    def _(step):
        q_copy(me, at_z(step, y), step).start()

    q_copy(me, across, 0).start()
    q_copy(me, sibling, depth).start()

    @pl.loop(1, depth)
    def _(step):
        source = at_z(depth - step, y)
        q_copy(source, sibling, 0).wait_recv()
        q_copy(source, across, 2 * depth + step).start()
        q_copy(source, sibling, depth + step).start()

    @pl.loop(0, depth)
    def _(step):
        source = at_z(depth - step, 1 - y)
        q_copy(source, sibling, 0).wait_recv()
        q_copy(source, sibling, 3 * depth + step).start()

    @pl.loop(0, n // 2)
    def _(step):
        q_copy(2 * step + 1 - core, sibling, 0).wait_recv()

    def part_copy(h, p, source):
        slot = h * owners + p
        return (
            pltpu.make_async_remote_copy(
                src_ref=part_out.at[h],
                dst_ref=part_in.at[source],
                send_sem=p_send.at[slot],
                recv_sem=p_recv.at[source],
                device_id={"ctx": slot},
                device_id_type=MESH,
            ),
            pltpu.make_async_remote_copy(
                src_ref=stat_out.at[h],
                dst_ref=stat_in.at[source],
                send_sem=s_send.at[slot],
                recv_sem=s_recv.at[source],
                device_id={"ctx": slot},
                device_id_type=MESH,
            ),
        )

    tile = chunk_of(context, 512)

    def queries_of(h):
        return q_all[:, h].astype(f32).reshape(rows, head_dim).astype(bf16)

    def merged(peaks, totals, parts):
        peak = functools.reduce(jnp.maximum, peaks)
        factors = [jnp.exp2(p - peak) for p in peaks]
        total = sum(f * t for f, t in zip(factors, totals))
        return peak, total, sum(f * w for f, w in zip(factors, parts))

    @pl.loop(0, kv_heads // 2)
    def _(step):
        heads = [head_at(2 * step), head_at(2 * step + 1)]
        empty = jnp.zeros((rows, head_dim), bf16)
        q0, q1 = [queries_of(h) for h in heads]
        q = jnp.concatenate(
            [jnp.concatenate([q0, empty], axis=1), jnp.concatenate([empty, q1], axis=1)], axis=0
        )
        for h in heads:
            k_copy(h).wait()
            v_copy(h).wait()
        peaks, totals, parts = ([], []), ([], []), ([], [])
        for t in range(0, context, tile):
            at = pl.ds(t, tile)
            scores = lax.dot_general(
                jnp.concatenate([k_buf[h, at, :] for h in heads], axis=1),
                q,
                (((1,), (1,)), ((), ())),
                preferred_element_type=f32,
            )
            peak = jnp.max(scores, axis=0, keepdims=True) * scale
            exponent = jnp.exp2(scores * scale - peak)
            total = jnp.sum(exponent, axis=0, keepdims=True)
            weights = exponent.astype(bf16)
            for i, h in enumerate(heads):
                mine = slice(i * rows, (i + 1) * rows)
                peaks[i].append(peak[:, mine])
                totals[i].append(total[:, mine])
                parts[i].append(
                    lax.dot_general(
                        v_buf[h, at, :],
                        weights[:, mine],
                        (((0,), (0,)), ((), ())),
                        preferred_element_type=f32,
                    )
                )
        row = lax.broadcasted_iota(jnp.int32, (8, rows), 0)
        for i, h in enumerate(heads):
            peak, total, weighted = merged(peaks[i], totals[i], parts[i])
            part_out[h] = weighted.astype(bf16)
            stat_out[h] = jnp.where(row == 0, peak, total)
            for p in range(owners):

                @pl.when(h * owners + p != me)
                def _():
                    for copy in part_copy(h, p, me):
                        copy.start()

    part_in[me] = part_out[own_head]
    stat_in[me] = stat_out[own_head]

    @pl.loop(1, n)
    def _(step):
        for copy in part_copy(0, 0, lax.rem(me + step, n)):
            copy.wait_recv()

    stats = stat_in[...]
    overall = jnp.max(stats, axis=0)[0:1, :]
    total = jnp.zeros((1, rows), f32)
    weighted = jnp.zeros((head_dim, rows), f32)
    for k in range(n):
        factor = jnp.exp2(stats[k, 0:1, :] - overall)
        total += factor * stats[k, 1:2, :]
        weighted += factor * part_in[k].astype(f32)
    attended = (weighted / total).astype(bf16)

    unit = lax.broadcasted_iota(jnp.int32, (units, rows), 0)
    column = lax.broadcasted_iota(jnp.int32, (units, rows), 1)
    first = lax.rem(me, owners) * own_heads
    blocks = []
    for g in range(own_heads):
        place = (
            lax.div(unit, own_units) * own_rows + (first + g) * own_units + lax.rem(unit, own_units)
        )
        pick = jnp.where(column == place, 1.0, 0.0).astype(bf16)
        blocks.append(
            lax.dot_general(
                pick, attended, (((1,), (1,)), ((), ())), preferred_element_type=f32
            ).astype(bf16)
        )
    own_block = jnp.concatenate(blocks, axis=1) if own_heads > 1 else blocks[0]

    w_copy.wait()

    def core_copy(c):
        return pltpu.make_async_remote_copy(
            src_ref=y_out.at[c, 1 - core],
            dst_ref=core_in.at[c],
            send_sem=y_send.at[0, c],
            recv_sem=y_recv.at[0, c],
            device_id={"ctx": sibling},
            device_id_type=MESH,
        )

    def across_copy(c):
        return pltpu.make_async_remote_copy(
            src_ref=across_out.at[c],
            dst_ref=across_in.at[c],
            send_sem=y_send.at[1, c],
            recv_sem=y_recv.at[1, c],
            device_id={"ctx": across},
            device_id_type=MESH,
        )

    def z_copy(c, target, source):
        return pltpu.make_async_remote_copy(
            src_ref=z_out.at[c, target],
            dst_ref=z_in.at[c, source],
            send_sem=z_send.at[c, target],
            recv_sem=z_recv.at[c, source],
            device_id={"ctx": device(target, y, core)},
            device_id_type=MESH,
        )

    chunks = y_out.shape[0]
    cols = y_out.shape[-1]
    for c in range(chunks):
        product = jnp.dot(
            own_block, w_buf[:, c * cols : (c + 1) * cols], preferred_element_type=f32
        )
        for k in range(n):
            y_out[c, k % 2, k // 2 % 2, k // 4] = product[
                k * own_units : (k + 1) * own_units
            ].astype(bf16)
        core_copy(c).start()
    for c in range(chunks):
        core_copy(c).wait_recv()
        across_out[c] = (
            y_out[c, core, 1 - y].astype(f32) + core_in[c, 1 - y].astype(f32)
        ).astype(bf16)
        across_copy(c).start()
    for c in range(chunks):
        own_sum = y_out[c, core, y].astype(f32) + core_in[c, y].astype(f32)
        across_copy(c).wait_recv()
        z_out[c] = (own_sum + across_in[c].astype(f32)).astype(bf16)

        @pl.loop(1, depth)
        def _(step):
            z_copy(c, lax.rem(z + step, depth), z).start()

        z_in[c, z] = z_out[c, z]
    branches = []
    for c in range(chunks):

        @pl.loop(1, depth)
        def _(step):
            z_copy(c, z, lax.rem(z + step, depth)).wait_recv()

        branches.append(jnp.sum(z_in[c].astype(f32), axis=0))
    squares = sum(jnp.sum(b * b, axis=1, keepdims=True) for b in branches)
    inverse = lax.rsqrt(squares / width + 1e-06)
    for c, branch in enumerate(branches):
        at = pl.ds(c * cols, cols)
        gain = gain_ref[at].reshape(1, cols)
        out_ref[:, at] = res_ref[:, at].astype(f32) + branch * inverse * gain

    @pl.loop(0, n)
    def _(step):
        @pl.when(step != 2 * depth)
        def _():
            q_copy(me, sibling, step).wait_send()

    @pl.loop(1, n)
    def _(step):
        target = lax.rem(me + step, n)
        for copy in part_copy(lax.div(target, owners), lax.rem(target, owners), me):
            copy.wait_send()

    for c in range(chunks):
        core_copy(c).wait_send()
        across_copy(c).wait_send()

        @pl.loop(1, depth)
        def _(step):
            z_copy(c, lax.rem(z + step, depth), z).wait_send()


def shards(n, queries, keys, values, residual, post_gain, out_weight):
    kv_heads, context, head_dim = keys.shape
    own_units, all_width = queries.shape
    head_count = all_width // head_dim
    group_size = head_count // kv_heads
    own_rows = own_units * group_size
    rows = n * own_rows
    width = residual.shape[1]
    cols = chunk_of(width, 2048)
    chunks = width // cols
    depth = n // 4
    vmem = pl.BlockSpec(memory_space=pltpu.VMEM)
    hbm = pl.BlockSpec(memory_space=pl.ANY)
    dma = pltpu.SemaphoreType.DMA
    return pl.pallas_call(
        functools.partial(kernel, n, group_size),
        out_shape=jax.ShapeDtypeStruct((own_units, width), f32),
        in_specs=[vmem, hbm, hbm, vmem, vmem, hbm],
        out_specs=vmem,
        scratch_shapes=[
            pltpu.VMEM(keys.shape, bf16),
            pltpu.VMEM(values.shape, bf16),
            pltpu.VMEM(out_weight.shape, bf16),
            pltpu.VMEM((n, kv_heads, own_rows, head_dim), bf16),
            pltpu.VMEM((kv_heads, head_dim, rows), bf16),
            pltpu.VMEM((kv_heads, 8, rows), f32),
            pltpu.VMEM((n, head_dim, rows), bf16),
            pltpu.VMEM((n, 8, rows), f32),
            pltpu.VMEM((chunks, 2, 2, depth, own_units, cols), bf16),
            pltpu.VMEM((chunks, 2, depth, own_units, cols), bf16),
            pltpu.VMEM((chunks, depth, own_units, cols), bf16),
            pltpu.VMEM((chunks, depth, own_units, cols), bf16),
            pltpu.VMEM((chunks, depth, own_units, cols), bf16),
            pltpu.VMEM((chunks, depth, own_units, cols), bf16),
            dma((kv_heads,)),
            dma((kv_heads,)),
            dma,
            dma((n,)),
            dma((n,)),
            dma((n,)),
            dma((n,)),
            dma((n,)),
            dma((n,)),
            dma((2, chunks)),
            dma((2, chunks)),
            dma((chunks, depth)),
            dma((chunks, depth)),
        ],
        compiler_params=pltpu.CompilerParams(
            collective_id=0, has_side_effects=True, vmem_limit_bytes=56 * 2**20
        ),
        cost_estimate=pl.CostEstimate(
            flops=4 * kv_heads * context * rows * head_dim,
            bytes_accessed=4 * kv_heads * context * head_dim,
            transcendentals=kv_heads * context * rows,
        ),
    )(queries, keys, values, residual, post_gain, out_weight)


def solution(mesh):
    in_specs = (
        P(("groups", "ctx"), None),
        P(None, ("groups", "ctx"), None),
        P(None, ("groups", "ctx"), None),
        P(("groups", "ctx"), None),
        P(),
        P("ctx", None),
    )
    out_specs = P(("groups", "ctx"), None)
    return jax.shard_map(
        functools.partial(shards, mesh.shape["ctx"]),
        mesh=mesh,
        in_specs=in_specs,
        out_specs=out_specs,
        check_vma=False,
    )
```

```python
import functools
import math

import jax
import jax.numpy as jnp
from jax import lax
from jax.experimental import pallas as pl
from jax.experimental.pallas import tpu as pltpu
from jax.sharding import PartitionSpec as P

MESH = pl.DeviceIdType.MESH
f32, bf16 = jnp.float32, jnp.bfloat16


def chunk_of(extent, largest):
    return max(c for c in range(128, largest + 1, 128) if extent % c == 0)


def kernel(
    n,
    group_size,
    q_ref,
    k_hbm,
    v_hbm,
    res_ref,
    gain_ref,
    w_hbm,
    out_ref,
    k_buf,
    v_buf,
    w_buf,
    q_all,
    part_out,
    stat_out,
    part_in,
    stat_in,
    y_out,
    core_in,
    across_out,
    across_in,
    z_out,
    z_in,
    k_sem,
    v_sem,
    w_sem,
    q_send,
    q_recv,
    p_send,
    p_recv,
    s_send,
    s_recv,
    y_send,
    y_recv,
    z_send,
    z_recv,
):
    me = lax.axis_index("ctx")
    core = lax.rem(me, 2)
    sibling = me + 1 - 2 * core
    depth = n // 4
    y = lax.rem(lax.div(me, 2), 2)
    z = lax.div(me, 4)

    def device(its_z, its_y, its_core):
        return (its_z * 2 + its_y) * 2 + its_core

    across = device(z, 1 - y, core)
    kv_heads, context, head_dim = k_buf.shape
    own_units = q_ref.shape[0]
    owners = n // kv_heads
    own_heads = group_size // owners
    own_rows = own_units * group_size
    rows = n * own_rows
    units = n * own_units
    width = w_buf.shape[1]
    scale = 168.0**-0.5 * math.log2(math.e)
    own_head = lax.div(me, owners)

    def head_at(step):
        return lax.rem(own_head + 1 + step, kv_heads)

    def k_copy(h):
        return pltpu.make_async_copy(k_hbm.at[h], k_buf.at[h], k_sem.at[h])

    def v_copy(h):
        return pltpu.make_async_copy(v_hbm.at[h], v_buf.at[h], v_sem.at[h])

    w_copy = pltpu.make_async_copy(w_hbm, w_buf, w_sem)

    @pl.loop(0, kv_heads)
    def _(step):
        k_copy(head_at(step)).start()
        v_copy(head_at(step)).start()

    w_copy.start()

    barrier = pltpu.get_barrier_semaphore()

    @pl.loop(1, n)
    def _(step):
        pl.semaphore_signal(
            barrier, inc=1, device_id={"ctx": lax.rem(me + step, n)}, device_id_type=MESH
        )

    own = q_ref[...].astype(f32)
    for h in range(kv_heads):
        first = h * group_size * head_dim
        q_all[me, h] = jnp.concatenate(
            [own[:, first + g * head_dim :][:, :head_dim] for g in range(group_size)], axis=0
        ).astype(bf16)

    pl.semaphore_wait(barrier, n - 1)

    def q_copy(block, target, slot):
        return pltpu.make_async_remote_copy(
            src_ref=q_all.at[block],
            dst_ref=q_all.at[block],
            send_sem=q_send.at[slot],
            recv_sem=q_recv.at[block],
            device_id={"ctx": target},
            device_id_type=MESH,
        )

    def at_z(step, its_y):
        return device(lax.rem(z + step, depth), its_y, core)

    @pl.loop(1, depth)
    def _(step):
        q_copy(me, at_z(step, y), step).start()

    q_copy(me, across, 0).start()
    q_copy(me, sibling, depth).start()

    @pl.loop(1, depth)
    def _(step):
        source = at_z(depth - step, y)
        q_copy(source, sibling, 0).wait_recv()
        q_copy(source, across, 2 * depth + step).start()
        q_copy(source, sibling, depth + step).start()

    @pl.loop(0, depth)
    def _(step):
        source = at_z(depth - step, 1 - y)
        q_copy(source, sibling, 0).wait_recv()
        q_copy(source, sibling, 3 * depth + step).start()

    @pl.loop(0, n // 2)
    def _(step):
        q_copy(2 * step + 1 - core, sibling, 0).wait_recv()

    def part_copy(h, p, source):
        slot = h * owners + p
        return (
            pltpu.make_async_remote_copy(
                src_ref=part_out.at[h],
                dst_ref=part_in.at[source],
                send_sem=p_send.at[slot],
                recv_sem=p_recv.at[source],
                device_id={"ctx": slot},
                device_id_type=MESH,
            ),
            pltpu.make_async_remote_copy(
                src_ref=stat_out.at[h],
                dst_ref=stat_in.at[source],
                send_sem=s_send.at[slot],
                recv_sem=s_recv.at[source],
                device_id={"ctx": slot},
                device_id_type=MESH,
            ),
        )

    tile = chunk_of(context, 1024)

    def queries_of(h):
        return q_all[:, h].astype(f32).reshape(rows, head_dim).astype(bf16)

    def attend(h):
        q = queries_of(h)
        peaks, totals, parts = [], [], []
        for t in range(0, context, tile):
            at = pl.ds(t, tile)
            scores = lax.dot_general(
                q, k_buf[h, at, :], (((1,), (1,)), ((), ())), preferred_element_type=f32
            )
            peak = jnp.max(scores, axis=1, keepdims=True) * scale
            exponent = jnp.exp2(scores * scale - peak)
            peaks.append(peak)
            totals.append(jnp.sum(exponent, axis=1, keepdims=True))
            parts.append(
                jnp.dot(exponent.astype(bf16), v_buf[h, at, :], preferred_element_type=f32)
            )
        peak = functools.reduce(jnp.maximum, peaks)
        factors = [jnp.exp2(p - peak) for p in peaks]
        total = sum(f * t for f, t in zip(factors, totals))
        weighted = sum(f * w for f, w in zip(factors, parts))
        lane = lax.broadcasted_iota(jnp.int32, (rows, 128), 1)
        part_out[h] = weighted.astype(bf16)
        stat_out[h] = jnp.where(lane == 0, peak, total).T[0:8]

    @pl.loop(0, kv_heads // 2)
    def _(step):
        heads = [head_at(2 * step), head_at(2 * step + 1)]
        for h in heads:
            k_copy(h).wait()
            v_copy(h).wait()
        for h in heads:
            attend(h)
        for h in heads:
            for p in range(owners):

                @pl.when(h * owners + p != me)
                def _():
                    for copy in part_copy(h, p, me):
                        copy.start()

    part_in[me] = part_out[own_head]
    stat_in[me] = stat_out[own_head]

    @pl.loop(1, n)
    def _(step):
        for copy in part_copy(0, 0, lax.rem(me + step, n)):
            copy.wait_recv()

    peaks, totals = stat_in[:, 0, :], stat_in[:, 1, :]
    factors = jnp.exp2(peaks - jnp.max(peaks, axis=0, keepdims=True))
    shares = (factors / jnp.sum(factors * totals, axis=0, keepdims=True)).T
    attended = sum(shares[:, k : k + 1] * part_in[k].astype(f32) for k in range(n)).astype(bf16)

    unit = lax.broadcasted_iota(jnp.int32, (units, rows), 0)
    column = lax.broadcasted_iota(jnp.int32, (units, rows), 1)
    first = lax.rem(me, owners) * own_heads
    blocks = []
    for g in range(own_heads):
        place = (
            lax.div(unit, own_units) * own_rows + (first + g) * own_units + lax.rem(unit, own_units)
        )
        pick = jnp.where(column == place, 1.0, 0.0).astype(bf16)
        blocks.append(
            jnp.dot(pick, attended, preferred_element_type=f32).astype(bf16)
        )
    own_block = jnp.concatenate(blocks, axis=1) if own_heads > 1 else blocks[0]

    w_copy.wait()

    def core_copy(c):
        return pltpu.make_async_remote_copy(
            src_ref=y_out.at[c, 1 - core],
            dst_ref=core_in.at[c],
            send_sem=y_send.at[0, c],
            recv_sem=y_recv.at[0, c],
            device_id={"ctx": sibling},
            device_id_type=MESH,
        )

    def across_copy(c):
        return pltpu.make_async_remote_copy(
            src_ref=across_out.at[c],
            dst_ref=across_in.at[c],
            send_sem=y_send.at[1, c],
            recv_sem=y_recv.at[1, c],
            device_id={"ctx": across},
            device_id_type=MESH,
        )

    def z_copy(c, target, source):
        return pltpu.make_async_remote_copy(
            src_ref=z_out.at[c, target],
            dst_ref=z_in.at[c, source],
            send_sem=z_send.at[c, target],
            recv_sem=z_recv.at[c, source],
            device_id={"ctx": device(target, y, core)},
            device_id_type=MESH,
        )

    chunks = y_out.shape[0]
    cols = y_out.shape[-1]
    for c in range(chunks):
        product = jnp.dot(
            own_block, w_buf[:, c * cols : (c + 1) * cols], preferred_element_type=f32
        )
        for k in range(n):
            y_out[c, k % 2, k // 2 % 2, k // 4] = product[
                k * own_units : (k + 1) * own_units
            ].astype(bf16)
        core_copy(c).start()
    for c in range(chunks):
        core_copy(c).wait_recv()
        across_out[c] = (
            y_out[c, core, 1 - y].astype(f32) + core_in[c, 1 - y].astype(f32)
        ).astype(bf16)
        across_copy(c).start()
    for c in range(chunks):
        own_sum = y_out[c, core, y].astype(f32) + core_in[c, y].astype(f32)
        across_copy(c).wait_recv()
        z_out[c] = (own_sum + across_in[c].astype(f32)).astype(bf16)

        @pl.loop(1, depth)
        def _(step):
            z_copy(c, lax.rem(z + step, depth), z).start()

        z_in[c, z] = z_out[c, z]
    branches = []
    for c in range(chunks):

        @pl.loop(1, depth)
        def _(step):
            z_copy(c, z, lax.rem(z + step, depth)).wait_recv()

        branches.append(jnp.sum(z_in[c].astype(f32), axis=0))
    squares = sum(jnp.sum(b * b, axis=1, keepdims=True) for b in branches)
    inverse = lax.rsqrt(squares / width + 1e-06)
    for c, branch in enumerate(branches):
        at = pl.ds(c * cols, cols)
        gain = gain_ref[at].reshape(1, cols)
        out_ref[:, at] = res_ref[:, at].astype(f32) + branch * inverse * gain

    @pl.loop(0, n)
    def _(step):
        @pl.when(step != 2 * depth)
        def _():
            q_copy(me, sibling, step).wait_send()

    @pl.loop(1, n)
    def _(step):
        target = lax.rem(me + step, n)
        for copy in part_copy(lax.div(target, owners), lax.rem(target, owners), me):
            copy.wait_send()

    for c in range(chunks):
        core_copy(c).wait_send()
        across_copy(c).wait_send()

        @pl.loop(1, depth)
        def _(step):
            z_copy(c, lax.rem(z + step, depth), z).wait_send()


def shards(n, queries, keys, values, residual, post_gain, out_weight):
    kv_heads, context, head_dim = keys.shape
    own_units, all_width = queries.shape
    head_count = all_width // head_dim
    group_size = head_count // kv_heads
    own_rows = own_units * group_size
    rows = n * own_rows
    width = residual.shape[1]
    cols = chunk_of(width, 2048)
    chunks = width // cols
    depth = n // 4
    vmem = pl.BlockSpec(memory_space=pltpu.VMEM)
    hbm = pl.BlockSpec(memory_space=pl.ANY)
    dma = pltpu.SemaphoreType.DMA
    return pl.pallas_call(
        functools.partial(kernel, n, group_size),
        out_shape=jax.ShapeDtypeStruct((own_units, width), f32),
        in_specs=[vmem, hbm, hbm, vmem, vmem, hbm],
        out_specs=vmem,
        scratch_shapes=[
            pltpu.VMEM(keys.shape, bf16),
            pltpu.VMEM(values.shape, bf16),
            pltpu.VMEM(out_weight.shape, bf16),
            pltpu.VMEM((n, kv_heads, own_rows, head_dim), bf16),
            pltpu.VMEM((kv_heads, rows, head_dim), bf16),
            pltpu.VMEM((kv_heads, 8, rows), f32),
            pltpu.VMEM((n, rows, head_dim), bf16),
            pltpu.VMEM((n, 8, rows), f32),
            pltpu.VMEM((chunks, 2, 2, depth, own_units, cols), bf16),
            pltpu.VMEM((chunks, 2, depth, own_units, cols), bf16),
            pltpu.VMEM((chunks, depth, own_units, cols), bf16),
            pltpu.VMEM((chunks, depth, own_units, cols), bf16),
            pltpu.VMEM((chunks, depth, own_units, cols), bf16),
            pltpu.VMEM((chunks, depth, own_units, cols), bf16),
            dma((kv_heads,)),
            dma((kv_heads,)),
            dma,
            dma((n,)),
            dma((n,)),
            dma((n,)),
            dma((n,)),
            dma((n,)),
            dma((n,)),
            dma((2, chunks)),
            dma((2, chunks)),
            dma((chunks, depth)),
            dma((chunks, depth)),
        ],
        compiler_params=pltpu.CompilerParams(
            collective_id=0, has_side_effects=True, vmem_limit_bytes=56 * 2**20
        ),
        cost_estimate=pl.CostEstimate(
            flops=4 * kv_heads * context * rows * head_dim,
            bytes_accessed=4 * kv_heads * context * head_dim,
            transcendentals=kv_heads * context * rows,
        ),
    )(queries, keys, values, residual, post_gain, out_weight)


def solution(mesh):
    in_specs = (
        P(("groups", "ctx"), None),
        P(None, ("groups", "ctx"), None),
        P(None, ("groups", "ctx"), None),
        P(("groups", "ctx"), None),
        P(),
        P("ctx", None),
    )
    out_specs = P(("groups", "ctx"), None)
    return jax.shard_map(
        functools.partial(shards, mesh.shape["ctx"]),
        mesh=mesh,
        in_specs=in_specs,
        out_specs=out_specs,
        check_vma=False,
    )
```

```python
import functools
import math

import jax
import jax.numpy as jnp
from jax import lax
from jax.experimental import pallas as pl
from jax.experimental.pallas import tpu as pltpu
from jax.sharding import PartitionSpec as P

MESH = pl.DeviceIdType.MESH
f32, bf16 = jnp.float32, jnp.bfloat16


def chunk_of(extent, largest):
    return max(c for c in range(128, largest + 1, 128) if extent % c == 0)


def kernel(
    n,
    group_size,
    q_ref,
    k_hbm,
    v_hbm,
    res_ref,
    gain_ref,
    w_hbm,
    out_ref,
    k_buf,
    v_buf,
    w_buf,
    q_all,
    core_out,
    core_got,
    cross_out,
    cross_got,
    deep_out,
    deep_got,
    mine_weighted,
    mine_stat,
    y_out,
    core_in,
    across_out,
    across_in,
    z_out,
    z_in,
    k_sem,
    v_sem,
    w_sem,
    q_send,
    q_recv,
    p_send,
    p_recv,
    y_send,
    y_recv,
    z_send,
    z_recv,
):
    me = lax.axis_index("ctx")
    core = lax.rem(me, 2)
    sibling = me + 1 - 2 * core
    depth = n // 4
    y = lax.rem(lax.div(me, 2), 2)
    z = lax.div(me, 4)

    def device(its_z, its_y, its_core):
        return (its_z * 2 + its_y) * 2 + its_core

    across = device(z, 1 - y, core)
    kv_heads, context, head_dim = k_buf.shape
    own_units = q_ref.shape[0]
    owners = n // kv_heads
    own_heads = group_size // owners
    own_rows = own_units * group_size
    rows = n * own_rows
    units = n * own_units
    width = w_buf.shape[1]
    scale = 168.0**-0.5 * math.log2(math.e)
    chips = n // 2

    def place_at(rank):
        its_y = jnp.where(rank < depth, 1 - y, y)
        return lax.rem(z + 1 + rank, depth), its_y

    def head_at(step):
        rank = lax.rem(step, chips)
        its_z, its_y = place_at(rank)
        chip = its_z * 2 + its_y
        if owners > 1:
            return chip
        return chip * 2 + jnp.where(step < chips, 1 - core, core)

    def k_copy(h):
        return pltpu.make_async_copy(k_hbm.at[h], k_buf.at[h], k_sem.at[h])

    def v_copy(h):
        return pltpu.make_async_copy(v_hbm.at[h], v_buf.at[h], v_sem.at[h])

    w_copy = pltpu.make_async_copy(w_hbm, w_buf, w_sem)

    @pl.loop(0, kv_heads)
    def _(step):
        k_copy(head_at(step)).start()
        v_copy(head_at(step)).start()

    w_copy.start()

    barrier = pltpu.get_barrier_semaphore()

    def greet(target):
        pl.semaphore_signal(barrier, inc=1, device_id={"ctx": target}, device_id_type=MESH)

    greet(sibling)
    greet(across)

    @pl.loop(1, depth)
    def _(step):
        greet(device(lax.rem(z + step, depth), y, core))

    own = q_ref[...].astype(f32)
    for h in range(kv_heads):
        first = h * group_size * head_dim
        q_all[me, h] = jnp.concatenate(
            [own[:, first + g * head_dim :][:, :head_dim] for g in range(group_size)], axis=0
        ).astype(bf16)

    pl.semaphore_wait(barrier, depth + 1)

    def q_copy(block, target, slot):
        return pltpu.make_async_remote_copy(
            src_ref=q_all.at[block],
            dst_ref=q_all.at[block],
            send_sem=q_send.at[slot],
            recv_sem=q_recv.at[block],
            device_id={"ctx": target},
            device_id_type=MESH,
        )

    def at_z(step, its_y):
        return device(lax.rem(z + step, depth), its_y, core)

    @pl.loop(1, depth)
    def _(step):
        q_copy(me, at_z(step, y), step).start()

    q_copy(me, across, 0).start()
    q_copy(me, sibling, depth).start()

    @pl.loop(1, depth)
    def _(step):
        source = at_z(depth - step, y)
        q_copy(source, sibling, 0).wait_recv()
        q_copy(source, across, 2 * depth + step).start()
        q_copy(source, sibling, depth + step).start()

    @pl.loop(0, depth)
    def _(step):
        source = at_z(depth - step, 1 - y)
        q_copy(source, sibling, 0).wait_recv()
        q_copy(source, sibling, 3 * depth + step).start()

    @pl.loop(0, n // 2)
    def _(step):
        q_copy(2 * step + 1 - core, sibling, 0).wait_recv()

    def part_copies(target, out, into, kind, slot, landing):
        return [
            pltpu.make_async_remote_copy(
                src_ref=source,
                dst_ref=destination,
                send_sem=p_send.at[kind, i, slot],
                recv_sem=p_recv.at[kind, i, landing],
                device_id={"ctx": target},
                device_id_type=MESH,
            )
            for i, (source, destination) in enumerate(zip(out, into))
        ]

    def at(refs, i):
        return [ref.at[i] for ref in refs]

    def to_core(chip):
        return part_copies(sibling, at(core_out, chip), at(core_got, chip), 0, chip, chip)

    def to_across(its_z):
        return part_copies(across, at(cross_out, its_z), at(cross_got, its_z), 1, its_z, its_z)

    def to_z(target, source):
        return part_copies(
            device(target, y, core), at(deep_out, target), at(deep_got, source), 2, target, source
        )

    def start(copies):
        for copy in copies:
            copy.start()

    def put(refs, i, partial):
        peak, total, weighted = partial
        row = lax.broadcasted_iota(jnp.int32, (8, rows), 0)
        refs[0][i] = weighted.astype(bf16)
        refs[1][i] = jnp.where(row == 0, peak, total)

    def get(refs, i):
        return refs[1][i, 0:1, :], refs[1][i, 1:2, :], refs[0][i].astype(f32)

    def merge(partials):
        peak = functools.reduce(jnp.maximum, [p for p, _, _ in partials])
        factors = [jnp.exp2(p - peak) for p, _, _ in partials]
        total = sum(f * t for f, (_, t, _) in zip(factors, partials))
        return peak, total, sum(f * w for f, (_, _, w) in zip(factors, partials))

    tile = chunk_of(context, 512)

    @pl.loop(0, kv_heads)
    def _(step):
        h = head_at(step)
        rank = lax.rem(step, chips)
        its_z, its_y = place_at(rank)
        chip = its_z * 2 + its_y
        q = q_all[:, h].astype(f32).reshape(rows, head_dim).astype(bf16)
        k_copy(h).wait()
        v_copy(h).wait()
        partials = []
        for t in range(0, context, tile):
            scores = lax.dot_general(
                k_buf[h, pl.ds(t, tile), :],
                q,
                (((1,), (1,)), ((), ())),
                preferred_element_type=f32,
            )
            peak = jnp.max(scores, axis=0, keepdims=True) * scale
            exponent = jnp.exp2(scores * scale - peak)
            total = jnp.sum(exponent, axis=0, keepdims=True)
            weighted = lax.dot_general(
                v_buf[h, pl.ds(t, tile), :],
                exponent.astype(bf16),
                (((0,), (0,)), ((), ())),
                preferred_element_type=f32,
            )
            partials.append((peak, total, weighted))
        peak, total, weighted = merge(partials)
        mine_weighted[...] = weighted
        mine_stat[0:1, :] = peak
        mine_stat[1:2, :] = total

        def mine():
            return mine_stat[0:1, :], mine_stat[1:2, :], mine_weighted[...]

        @pl.when((step < chips) if owners == 1 else (step >= 0))
        def _():
            put(core_out, chip, mine())
            start(to_core(chip))

        @pl.when((step >= chips) if owners == 1 else (step >= 0))
        def _():
            for copy in to_core(chip):
                copy.wait_recv()
            two = merge([mine(), get(core_got, chip)])

            @pl.when(rank < depth)
            def _():
                put(cross_out, its_z, two)
                start(to_across(its_z))

            @pl.when(rank >= depth)
            def _():
                for copy in to_across(its_z):
                    copy.wait_recv()
                put(deep_out, its_z, merge([two, get(cross_got, its_z)]))

                @pl.when(its_z != z)
                def _():
                    start(to_z(its_z, z))

    deep_got[0][z] = deep_out[0][z]
    deep_got[1][z] = deep_out[1][z]

    @pl.loop(1, depth)
    def _(step):
        for copy in to_z(z, lax.rem(z + step, depth)):
            copy.wait_recv()

    _, total, weighted = merge([get(deep_got, i) for i in range(depth)])
    attended = (weighted / total).astype(bf16)

    unit = lax.broadcasted_iota(jnp.int32, (units, rows), 0)
    column = lax.broadcasted_iota(jnp.int32, (units, rows), 1)
    first = lax.rem(me, owners) * own_heads
    blocks = []
    for g in range(own_heads):
        place = (
            lax.div(unit, own_units) * own_rows + (first + g) * own_units + lax.rem(unit, own_units)
        )
        pick = jnp.where(column == place, 1.0, 0.0).astype(bf16)
        blocks.append(
            lax.dot_general(
                pick, attended, (((1,), (1,)), ((), ())), preferred_element_type=f32
            ).astype(bf16)
        )
    own_block = jnp.concatenate(blocks, axis=1) if own_heads > 1 else blocks[0]

    w_copy.wait()

    def core_copy(c):
        return pltpu.make_async_remote_copy(
            src_ref=y_out.at[c, 1 - core],
            dst_ref=core_in.at[c],
            send_sem=y_send.at[0, c],
            recv_sem=y_recv.at[0, c],
            device_id={"ctx": sibling},
            device_id_type=MESH,
        )

    def across_copy(c):
        return pltpu.make_async_remote_copy(
            src_ref=across_out.at[c],
            dst_ref=across_in.at[c],
            send_sem=y_send.at[1, c],
            recv_sem=y_recv.at[1, c],
            device_id={"ctx": across},
            device_id_type=MESH,
        )

    def z_copy(c, target, source):
        return pltpu.make_async_remote_copy(
            src_ref=z_out.at[c, target],
            dst_ref=z_in.at[c, source],
            send_sem=z_send.at[c, target],
            recv_sem=z_recv.at[c, source],
            device_id={"ctx": device(target, y, core)},
            device_id_type=MESH,
        )

    chunks = y_out.shape[0]
    cols = y_out.shape[-1]
    for c in range(chunks):
        product = jnp.dot(
            own_block, w_buf[:, c * cols : (c + 1) * cols], preferred_element_type=f32
        )
        for k in range(n):
            y_out[c, k % 2, k // 2 % 2, k // 4] = product[
                k * own_units : (k + 1) * own_units
            ].astype(bf16)
        core_copy(c).start()
    for c in range(chunks):
        core_copy(c).wait_recv()
        across_out[c] = (
            y_out[c, core, 1 - y].astype(f32) + core_in[c, 1 - y].astype(f32)
        ).astype(bf16)
        across_copy(c).start()
    for c in range(chunks):
        own_sum = y_out[c, core, y].astype(f32) + core_in[c, y].astype(f32)
        across_copy(c).wait_recv()
        z_out[c] = (own_sum + across_in[c].astype(f32)).astype(bf16)

        @pl.loop(1, depth)
        def _(step):
            z_copy(c, lax.rem(z + step, depth), z).start()

        z_in[c, z] = z_out[c, z]
    branches = []
    for c in range(chunks):

        @pl.loop(1, depth)
        def _(step):
            z_copy(c, z, lax.rem(z + step, depth)).wait_recv()

        branches.append(jnp.sum(z_in[c].astype(f32), axis=0))
    squares = sum(jnp.sum(b * b, axis=1, keepdims=True) for b in branches)
    inverse = lax.rsqrt(squares / width + 1e-06)
    for c, branch in enumerate(branches):
        span = pl.ds(c * cols, cols)
        gain = gain_ref[span].reshape(1, cols)
        out_ref[:, span] = res_ref[:, span].astype(f32) + branch * inverse * gain

    @pl.loop(0, n)
    def _(step):
        @pl.when(step != 2 * depth)
        def _():
            q_copy(me, sibling, step).wait_send()

    @pl.loop(0, chips)
    def _(chip):
        for copy in to_core(chip):
            copy.wait_send()

    @pl.loop(0, depth)
    def _(its_z):
        for copy in to_across(its_z):
            copy.wait_send()

        @pl.when(its_z != z)
        def _():
            for copy in to_z(its_z, z):
                copy.wait_send()

    for c in range(chunks):
        core_copy(c).wait_send()
        across_copy(c).wait_send()

        @pl.loop(1, depth)
        def _(step):
            z_copy(c, lax.rem(z + step, depth), z).wait_send()


def shards(n, queries, keys, values, residual, post_gain, out_weight):
    kv_heads, context, head_dim = keys.shape
    own_units, all_width = queries.shape
    head_count = all_width // head_dim
    group_size = head_count // kv_heads
    own_rows = own_units * group_size
    rows = n * own_rows
    width = residual.shape[1]
    cols = chunk_of(width, 2048)
    chunks = width // cols
    depth = n // 4
    vmem = pl.BlockSpec(memory_space=pltpu.VMEM)
    hbm = pl.BlockSpec(memory_space=pl.ANY)
    dma = pltpu.SemaphoreType.DMA

    def partials(count):
        return [
            pltpu.VMEM((count, head_dim, rows), bf16),
            pltpu.VMEM((count, 8, rows), f32),
        ]

    return pl.pallas_call(
        functools.partial(kernel, n, group_size),
        out_shape=jax.ShapeDtypeStruct((own_units, width), f32),
        in_specs=[vmem, hbm, hbm, vmem, vmem, hbm],
        out_specs=vmem,
        scratch_shapes=[
            pltpu.VMEM(keys.shape, bf16),
            pltpu.VMEM(values.shape, bf16),
            pltpu.VMEM(out_weight.shape, bf16),
            pltpu.VMEM((n, kv_heads, own_rows, head_dim), bf16),
            partials(n // 2),
            partials(n // 2),
            partials(depth),
            partials(depth),
            partials(depth),
            partials(depth),
            pltpu.VMEM((head_dim, rows), f32),
            pltpu.VMEM((8, rows), f32),
            pltpu.VMEM((chunks, 2, 2, depth, own_units, cols), bf16),
            pltpu.VMEM((chunks, 2, depth, own_units, cols), bf16),
            pltpu.VMEM((chunks, depth, own_units, cols), bf16),
            pltpu.VMEM((chunks, depth, own_units, cols), bf16),
            pltpu.VMEM((chunks, depth, own_units, cols), bf16),
            pltpu.VMEM((chunks, depth, own_units, cols), bf16),
            dma((kv_heads,)),
            dma((kv_heads,)),
            dma,
            dma((n,)),
            dma((n,)),
            dma((3, 2, n // 2)),
            dma((3, 2, n // 2)),
            dma((2, chunks)),
            dma((2, chunks)),
            dma((chunks, depth)),
            dma((chunks, depth)),
        ],
        compiler_params=pltpu.CompilerParams(
            collective_id=0, has_side_effects=True, vmem_limit_bytes=56 * 2**20
        ),
        cost_estimate=pl.CostEstimate(
            flops=4 * kv_heads * context * rows * head_dim,
            bytes_accessed=4 * kv_heads * context * head_dim,
            transcendentals=kv_heads * context * rows,
        ),
    )(queries, keys, values, residual, post_gain, out_weight)


def solution(mesh):
    in_specs = (
        P(("groups", "ctx"), None),
        P(None, ("groups", "ctx"), None),
        P(None, ("groups", "ctx"), None),
        P(("groups", "ctx"), None),
        P(),
        P("ctx", None),
    )
    out_specs = P(("groups", "ctx"), None)
    return jax.shard_map(
        functools.partial(shards, mesh.shape["ctx"]),
        mesh=mesh,
        in_specs=in_specs,
        out_specs=out_specs,
        check_vma=False,
    )
```

```python
import functools
import math

import jax
import jax.numpy as jnp
from jax import lax
from jax.experimental import pallas as pl
from jax.experimental.pallas import tpu as pltpu
from jax.sharding import PartitionSpec as P

MESH = pl.DeviceIdType.MESH
f32, bf16 = jnp.float32, jnp.bfloat16


def chunk_of(extent, largest):
    return max(c for c in range(128, largest + 1, 128) if extent % c == 0)


def kernel(
    n,
    group_size,
    q_ref,
    k_hbm,
    v_hbm,
    res_ref,
    gain_ref,
    w_hbm,
    out_ref,
    k_buf,
    v_buf,
    w_buf,
    q_all,
    core_out,
    core_got,
    cross_out,
    cross_got,
    deep_out,
    deep_got,
    mine_weighted,
    mine_stat,
    y_out,
    core_in,
    across_out,
    across_in,
    z_out,
    z_in,
    k_sem,
    v_sem,
    w_sem,
    q_send,
    q_recv,
    p_send,
    p_recv,
    y_send,
    y_recv,
    z_send,
    z_recv,
):
    me = lax.axis_index("ctx")
    core = lax.rem(me, 2)
    sibling = me + 1 - 2 * core
    depth = n // 4
    y = lax.rem(lax.div(me, 2), 2)
    z = lax.div(me, 4)

    def device(its_z, its_y, its_core):
        return (its_z * 2 + its_y) * 2 + its_core

    across = device(z, 1 - y, core)
    kv_heads, context, head_dim = k_buf.shape
    own_units = q_ref.shape[0]
    owners = n // kv_heads
    own_heads = group_size // owners
    own_rows = own_units * group_size
    rows = n * own_rows
    units = n * own_units
    width = w_buf.shape[1]
    scale = 168.0**-0.5 * math.log2(math.e)
    chips = n // 2

    def place_at(rank):
        its_y = jnp.where(rank < depth, 1 - y, y)
        return lax.rem(z + 1 + rank, depth), its_y

    def head_at(step):
        rank = lax.rem(step, chips)
        its_z, its_y = place_at(rank)
        chip = its_z * 2 + its_y
        if owners > 1:
            return chip
        return chip * 2 + jnp.where(step < chips, 1 - core, core)

    def k_copy(h):
        return pltpu.make_async_copy(k_hbm.at[h], k_buf.at[h], k_sem.at[h])

    def v_copy(h):
        return pltpu.make_async_copy(v_hbm.at[h], v_buf.at[h], v_sem.at[h])

    w_copy = pltpu.make_async_copy(w_hbm, w_buf, w_sem)

    def load(step):
        k_copy(head_at(step)).start()
        v_copy(head_at(step)).start()

    first_loads = min(3, kv_heads)
    ahead = min(first_loads + 3, kv_heads)

    @pl.loop(0, first_loads)
    def _(step):
        load(step)

    barrier = pltpu.get_barrier_semaphore()

    def greet(target):
        pl.semaphore_signal(barrier, inc=1, device_id={"ctx": target}, device_id_type=MESH)

    greet(sibling)
    greet(across)

    @pl.loop(1, depth)
    def _(step):
        greet(device(lax.rem(z + step, depth), y, core))

    own = q_ref[...].astype(f32)
    for h in range(kv_heads):
        first = h * group_size * head_dim
        q_all[me, h] = jnp.concatenate(
            [own[:, first + g * head_dim :][:, :head_dim] for g in range(group_size)], axis=0
        ).astype(bf16)

    pl.semaphore_wait(barrier, depth + 1)

    def q_copy(block, target, slot):
        return pltpu.make_async_remote_copy(
            src_ref=q_all.at[block],
            dst_ref=q_all.at[block],
            send_sem=q_send.at[slot],
            recv_sem=q_recv.at[block],
            device_id={"ctx": target},
            device_id_type=MESH,
        )

    def at_z(step, its_y):
        return device(lax.rem(z + step, depth), its_y, core)

    @pl.loop(1, depth)
    def _(step):
        q_copy(me, at_z(step, y), step).start()

    q_copy(me, across, 0).start()
    q_copy(me, sibling, depth).start()

    @pl.loop(first_loads, ahead)
    def _(step):
        load(step)

    @pl.loop(1, depth)
    def _(step):
        source = at_z(depth - step, y)
        q_copy(source, sibling, 0).wait_recv()
        q_copy(source, across, 2 * depth + step).start()
        q_copy(source, sibling, depth + step).start()

    @pl.loop(0, depth)
    def _(step):
        source = at_z(depth - step, 1 - y)
        q_copy(source, sibling, 0).wait_recv()
        q_copy(source, sibling, 3 * depth + step).start()

    @pl.loop(0, n // 2)
    def _(step):
        q_copy(2 * step + 1 - core, sibling, 0).wait_recv()

    def part_copies(target, out, into, kind, slot, landing):
        return [
            pltpu.make_async_remote_copy(
                src_ref=source,
                dst_ref=destination,
                send_sem=p_send.at[kind, i, slot],
                recv_sem=p_recv.at[kind, i, landing],
                device_id={"ctx": target},
                device_id_type=MESH,
            )
            for i, (source, destination) in enumerate(zip(out, into))
        ]

    def at(refs, i):
        return [ref.at[i] for ref in refs]

    def to_core(chip):
        return part_copies(sibling, at(core_out, chip), at(core_got, chip), 0, chip, chip)

    def to_across(its_z):
        return part_copies(across, at(cross_out, its_z), at(cross_got, its_z), 1, its_z, its_z)

    def to_z(target, source):
        return part_copies(
            device(target, y, core), at(deep_out, target), at(deep_got, source), 2, target, source
        )

    def start(copies):
        for copy in copies:
            copy.start()

    def put(refs, i, partial):
        peak, total, weighted = partial
        row = lax.broadcasted_iota(jnp.int32, (8, rows), 0)
        refs[0][i] = weighted.astype(bf16)
        refs[1][i] = jnp.where(row == 0, peak, total)

    def get(refs, i):
        return refs[1][i, 0:1, :], refs[1][i, 1:2, :], refs[0][i].astype(f32)

    def merge(partials):
        peak = functools.reduce(jnp.maximum, [p for p, _, _ in partials])
        factors = [jnp.exp2(p - peak) for p, _, _ in partials]
        total = sum(f * t for f, (_, t, _) in zip(factors, partials))
        return peak, total, sum(f * w for f, (_, _, w) in zip(factors, partials))

    tile = chunk_of(context, 512)

    @pl.loop(0, kv_heads)
    def _(step):
        @pl.when(step + ahead < kv_heads)
        def _():
            load(step + ahead)

        @pl.when(step == kv_heads // 2)
        def _():
            w_copy.start()

        h = head_at(step)
        rank = lax.rem(step, chips)
        its_z, its_y = place_at(rank)
        chip = its_z * 2 + its_y
        q = q_all[:, h].astype(f32).reshape(rows, head_dim).astype(bf16)
        k_copy(h).wait()
        v_copy(h).wait()
        partials = []
        for t in range(0, context, tile):
            scores = lax.dot_general(
                k_buf[h, pl.ds(t, tile), :],
                q,
                (((1,), (1,)), ((), ())),
                preferred_element_type=f32,
            )
            peak = jnp.max(scores, axis=0, keepdims=True) * scale
            exponent = jnp.exp2(scores * scale - peak)
            total = jnp.sum(exponent, axis=0, keepdims=True)
            weighted = lax.dot_general(
                v_buf[h, pl.ds(t, tile), :],
                exponent.astype(bf16),
                (((0,), (0,)), ((), ())),
                preferred_element_type=f32,
            )
            partials.append((peak, total, weighted))
        peak, total, weighted = merge(partials)
        mine_weighted[...] = weighted
        mine_stat[0:1, :] = peak
        mine_stat[1:2, :] = total

        def mine():
            return mine_stat[0:1, :], mine_stat[1:2, :], mine_weighted[...]

        @pl.when((step < chips) if owners == 1 else (step >= 0))
        def _():
            put(core_out, chip, mine())
            start(to_core(chip))

        @pl.when((step >= chips) if owners == 1 else (step >= 0))
        def _():
            for copy in to_core(chip):
                copy.wait_recv()
            two = merge([mine(), get(core_got, chip)])

            @pl.when(rank < depth)
            def _():
                put(cross_out, its_z, two)
                start(to_across(its_z))

            @pl.when(rank >= depth)
            def _():
                for copy in to_across(its_z):
                    copy.wait_recv()
                put(deep_out, its_z, merge([two, get(cross_got, its_z)]))

                @pl.when(its_z != z)
                def _():
                    start(to_z(its_z, z))

    deep_got[0][z] = deep_out[0][z]
    deep_got[1][z] = deep_out[1][z]

    @pl.loop(1, depth)
    def _(step):
        for copy in to_z(z, lax.rem(z + step, depth)):
            copy.wait_recv()

    _, total, weighted = merge([get(deep_got, i) for i in range(depth)])
    attended = (weighted / total).astype(bf16)

    unit = lax.broadcasted_iota(jnp.int32, (units, rows), 0)
    column = lax.broadcasted_iota(jnp.int32, (units, rows), 1)
    first = lax.rem(me, owners) * own_heads
    blocks = []
    for g in range(own_heads):
        place = (
            lax.div(unit, own_units) * own_rows + (first + g) * own_units + lax.rem(unit, own_units)
        )
        pick = jnp.where(column == place, 1.0, 0.0).astype(bf16)
        blocks.append(
            lax.dot_general(
                pick, attended, (((1,), (1,)), ((), ())), preferred_element_type=f32
            ).astype(bf16)
        )
    own_block = jnp.concatenate(blocks, axis=1) if own_heads > 1 else blocks[0]

    w_copy.wait()

    def core_copy(c):
        return pltpu.make_async_remote_copy(
            src_ref=y_out.at[c, 1 - core],
            dst_ref=core_in.at[c],
            send_sem=y_send.at[0, c],
            recv_sem=y_recv.at[0, c],
            device_id={"ctx": sibling},
            device_id_type=MESH,
        )

    def across_copy(c):
        return pltpu.make_async_remote_copy(
            src_ref=across_out.at[c],
            dst_ref=across_in.at[c],
            send_sem=y_send.at[1, c],
            recv_sem=y_recv.at[1, c],
            device_id={"ctx": across},
            device_id_type=MESH,
        )

    def z_copy(c, target, source):
        return pltpu.make_async_remote_copy(
            src_ref=z_out.at[c, target],
            dst_ref=z_in.at[c, source],
            send_sem=z_send.at[c, target],
            recv_sem=z_recv.at[c, source],
            device_id={"ctx": device(target, y, core)},
            device_id_type=MESH,
        )

    chunks = y_out.shape[0]
    cols = y_out.shape[-1]
    for c in range(chunks):
        product = jnp.dot(
            own_block, w_buf[:, c * cols : (c + 1) * cols], preferred_element_type=f32
        )
        for k in range(n):
            y_out[c, k % 2, k // 2 % 2, k // 4] = product[
                k * own_units : (k + 1) * own_units
            ].astype(bf16)
        core_copy(c).start()
    for c in range(chunks):
        core_copy(c).wait_recv()
        across_out[c] = (
            y_out[c, core, 1 - y].astype(f32) + core_in[c, 1 - y].astype(f32)
        ).astype(bf16)
        across_copy(c).start()
    for c in range(chunks):
        own_sum = y_out[c, core, y].astype(f32) + core_in[c, y].astype(f32)
        across_copy(c).wait_recv()
        z_out[c] = (own_sum + across_in[c].astype(f32)).astype(bf16)

        @pl.loop(1, depth)
        def _(step):
            z_copy(c, lax.rem(z + step, depth), z).start()

        z_in[c, z] = z_out[c, z]
    branches = []
    for c in range(chunks):

        @pl.loop(1, depth)
        def _(step):
            z_copy(c, z, lax.rem(z + step, depth)).wait_recv()

        branches.append(jnp.sum(z_in[c].astype(f32), axis=0))
    squares = sum(jnp.sum(b * b, axis=1, keepdims=True) for b in branches)
    inverse = lax.rsqrt(squares / width + 1e-06)
    for c, branch in enumerate(branches):
        span = pl.ds(c * cols, cols)
        gain = gain_ref[span].reshape(1, cols)
        out_ref[:, span] = res_ref[:, span].astype(f32) + branch * inverse * gain

    @pl.loop(0, n)
    def _(step):
        @pl.when(step != 2 * depth)
        def _():
            q_copy(me, sibling, step).wait_send()

    @pl.loop(0, chips)
    def _(chip):
        for copy in to_core(chip):
            copy.wait_send()

    @pl.loop(0, depth)
    def _(its_z):
        for copy in to_across(its_z):
            copy.wait_send()

        @pl.when(its_z != z)
        def _():
            for copy in to_z(its_z, z):
                copy.wait_send()

    for c in range(chunks):
        core_copy(c).wait_send()
        across_copy(c).wait_send()

        @pl.loop(1, depth)
        def _(step):
            z_copy(c, lax.rem(z + step, depth), z).wait_send()


def shards(n, queries, keys, values, residual, post_gain, out_weight):
    kv_heads, context, head_dim = keys.shape
    own_units, all_width = queries.shape
    head_count = all_width // head_dim
    group_size = head_count // kv_heads
    own_rows = own_units * group_size
    rows = n * own_rows
    width = residual.shape[1]
    cols = chunk_of(width, 2048)
    chunks = width // cols
    depth = n // 4
    vmem = pl.BlockSpec(memory_space=pltpu.VMEM)
    hbm = pl.BlockSpec(memory_space=pl.ANY)
    dma = pltpu.SemaphoreType.DMA

    def partials(count):
        return [
            pltpu.VMEM((count, head_dim, rows), bf16),
            pltpu.VMEM((count, 8, rows), f32),
        ]

    return pl.pallas_call(
        functools.partial(kernel, n, group_size),
        out_shape=jax.ShapeDtypeStruct((own_units, width), f32),
        in_specs=[vmem, hbm, hbm, vmem, vmem, hbm],
        out_specs=vmem,
        scratch_shapes=[
            pltpu.VMEM(keys.shape, bf16),
            pltpu.VMEM(values.shape, bf16),
            pltpu.VMEM(out_weight.shape, bf16),
            pltpu.VMEM((n, kv_heads, own_rows, head_dim), bf16),
            partials(n // 2),
            partials(n // 2),
            partials(depth),
            partials(depth),
            partials(depth),
            partials(depth),
            pltpu.VMEM((head_dim, rows), f32),
            pltpu.VMEM((8, rows), f32),
            pltpu.VMEM((chunks, 2, 2, depth, own_units, cols), bf16),
            pltpu.VMEM((chunks, 2, depth, own_units, cols), bf16),
            pltpu.VMEM((chunks, depth, own_units, cols), bf16),
            pltpu.VMEM((chunks, depth, own_units, cols), bf16),
            pltpu.VMEM((chunks, depth, own_units, cols), bf16),
            pltpu.VMEM((chunks, depth, own_units, cols), bf16),
            dma((kv_heads,)),
            dma((kv_heads,)),
            dma,
            dma((n,)),
            dma((n,)),
            dma((3, 2, n // 2)),
            dma((3, 2, n // 2)),
            dma((2, chunks)),
            dma((2, chunks)),
            dma((chunks, depth)),
            dma((chunks, depth)),
        ],
        compiler_params=pltpu.CompilerParams(
            collective_id=0, has_side_effects=True, vmem_limit_bytes=56 * 2**20
        ),
        cost_estimate=pl.CostEstimate(
            flops=4 * kv_heads * context * rows * head_dim,
            bytes_accessed=4 * kv_heads * context * head_dim,
            transcendentals=kv_heads * context * rows,
        ),
    )(queries, keys, values, residual, post_gain, out_weight)


def solution(mesh):
    in_specs = (
        P(("groups", "ctx"), None),
        P(None, ("groups", "ctx"), None),
        P(None, ("groups", "ctx"), None),
        P(("groups", "ctx"), None),
        P(),
        P("ctx", None),
    )
    out_specs = P(("groups", "ctx"), None)
    return jax.shard_map(
        functools.partial(shards, mesh.shape["ctx"]),
        mesh=mesh,
        in_specs=in_specs,
        out_specs=out_specs,
        check_vma=False,
    )
```

```python
import functools
import math

import jax
import jax.numpy as jnp
from jax import lax
from jax.experimental import pallas as pl
from jax.experimental.pallas import tpu as pltpu
from jax.sharding import PartitionSpec as P

MESH = pl.DeviceIdType.MESH
f32, bf16 = jnp.float32, jnp.bfloat16


def chunk_of(extent, largest):
    return max(c for c in range(128, largest + 1, 128) if extent % c == 0)


def kernel(
    n,
    group_size,
    q_ref,
    k_hbm,
    v_hbm,
    res_ref,
    gain_ref,
    w_hbm,
    out_ref,
    k_buf,
    v_buf,
    w_buf,
    q_all,
    core_out,
    core_got,
    cross_out,
    cross_got,
    deep_out,
    deep_got,
    mine_weighted,
    mine_stat,
    y_out,
    core_in,
    across_out,
    across_in,
    z_out,
    z_in,
    k_sem,
    v_sem,
    w_sem,
    q_send,
    q_recv,
    p_send,
    p_recv,
    y_send,
    y_recv,
    z_send,
    z_recv,
):
    me = lax.axis_index("ctx")
    core = lax.rem(me, 2)
    sibling = me + 1 - 2 * core
    depth = n // 4
    y = lax.rem(lax.div(me, 2), 2)
    z = lax.div(me, 4)

    def device(its_z, its_y, its_core):
        return (its_z * 2 + its_y) * 2 + its_core

    across = device(z, 1 - y, core)
    kv_heads, context, head_dim = k_buf.shape
    own_units = q_ref.shape[0]
    owners = n // kv_heads
    own_heads = group_size // owners
    own_rows = own_units * group_size
    rows = n * own_rows
    units = n * own_units
    width = w_buf.shape[1]
    scale = 168.0**-0.5 * math.log2(math.e)
    chips = n // 2

    def place_at(rank):
        its_y = jnp.where(rank < depth, 1 - y, y)
        return lax.rem(z + 1 + rank, depth), its_y

    def head_at(step):
        rank = lax.rem(step, chips)
        its_z, its_y = place_at(rank)
        chip = its_z * 2 + its_y
        if owners > 1:
            return chip
        return chip * 2 + jnp.where(step < chips, 1 - core, core)

    def k_copy(h):
        return pltpu.make_async_copy(k_hbm.at[h], k_buf.at[h], k_sem.at[h])

    def v_copy(h):
        return pltpu.make_async_copy(v_hbm.at[h], v_buf.at[h], v_sem.at[h])

    w_copy = pltpu.make_async_copy(w_hbm, w_buf, w_sem)

    def load(step):
        k_copy(head_at(step)).start()
        v_copy(head_at(step)).start()

    first_loads = min(3, kv_heads)
    ahead = min(first_loads + 3, kv_heads)

    @pl.loop(0, first_loads)
    def _(step):
        load(step)

    barrier = pltpu.get_barrier_semaphore()

    def greet(target):
        pl.semaphore_signal(barrier, inc=1, device_id={"ctx": target}, device_id_type=MESH)

    greet(sibling)
    greet(across)

    @pl.loop(1, depth)
    def _(step):
        greet(device(lax.rem(z + step, depth), y, core))

    own = q_ref[...].astype(f32)
    for h in range(kv_heads):
        first = h * group_size * head_dim
        q_all[me, h] = jnp.concatenate(
            [own[:, first + g * head_dim :][:, :head_dim] for g in range(group_size)], axis=0
        ).astype(bf16)

    pl.semaphore_wait(barrier, depth + 1)

    def q_copy(block, target, slot):
        return pltpu.make_async_remote_copy(
            src_ref=q_all.at[block],
            dst_ref=q_all.at[block],
            send_sem=q_send.at[slot],
            recv_sem=q_recv.at[block],
            device_id={"ctx": target},
            device_id_type=MESH,
        )

    def at_z(step, its_y):
        return device(lax.rem(z + step, depth), its_y, core)

    @pl.loop(1, depth)
    def _(step):
        q_copy(me, at_z(step, y), step).start()

    q_copy(me, across, 0).start()
    q_copy(me, sibling, depth).start()

    @pl.loop(first_loads, ahead)
    def _(step):
        load(step)

    @pl.loop(1, depth)
    def _(step):
        source = at_z(depth - step, y)
        q_copy(source, sibling, 0).wait_recv()
        q_copy(source, across, 2 * depth + step).start()
        q_copy(source, sibling, depth + step).start()

    @pl.loop(0, depth)
    def _(step):
        source = at_z(depth - step, 1 - y)
        q_copy(source, sibling, 0).wait_recv()
        q_copy(source, sibling, 3 * depth + step).start()

    @pl.loop(0, n // 2)
    def _(step):
        q_copy(2 * step + 1 - core, sibling, 0).wait_recv()

    def part_copies(target, out, into, kind, slot, landing):
        return [
            pltpu.make_async_remote_copy(
                src_ref=source,
                dst_ref=destination,
                send_sem=p_send.at[kind, i, slot],
                recv_sem=p_recv.at[kind, i, landing],
                device_id={"ctx": target},
                device_id_type=MESH,
            )
            for i, (source, destination) in enumerate(zip(out, into))
        ]

    def at(refs, i):
        return [ref.at[i] for ref in refs]

    def to_core(chip):
        return part_copies(sibling, at(core_out, chip), at(core_got, chip), 0, chip, chip)

    def to_across(its_z):
        return part_copies(across, at(cross_out, its_z), at(cross_got, its_z), 1, its_z, its_z)

    def to_z(target, source):
        return part_copies(
            device(target, y, core), at(deep_out, target), at(deep_got, source), 2, target, source
        )

    def start(copies):
        for copy in copies:
            copy.start()

    def put(refs, i, partial):
        peak, total, weighted = partial
        row = lax.broadcasted_iota(jnp.int32, (8, rows), 0)
        refs[0][i] = weighted.astype(bf16)
        refs[1][i] = jnp.where(row == 0, peak, total)

    def get(refs, i):
        return refs[1][i, 0:1, :], refs[1][i, 1:2, :], refs[0][i].astype(f32)

    def merge(partials):
        peak = functools.reduce(jnp.maximum, [p for p, _, _ in partials])
        factors = [jnp.exp2(p - peak) for p, _, _ in partials]
        total = sum(f * t for f, (_, t, _) in zip(factors, partials))
        return peak, total, sum(f * w for f, (_, _, w) in zip(factors, partials))

    tile = chunk_of(context, 512)

    @pl.loop(0, kv_heads)
    def _(step):
        @pl.when(step + ahead < kv_heads)
        def _():
            load(step + ahead)

        @pl.when(step == kv_heads // 2)
        def _():
            w_copy.start()

        h = head_at(step)
        rank = lax.rem(step, chips)
        its_z, its_y = place_at(rank)
        chip = its_z * 2 + its_y
        q = q_all[:, h].astype(f32).reshape(rows, head_dim).astype(bf16)
        k_copy(h).wait()
        v_copy(h).wait()
        partials = []
        for t in range(0, context, tile):
            scores = lax.dot_general(
                k_buf[h, pl.ds(t, tile), :],
                q,
                (((1,), (1,)), ((), ())),
                preferred_element_type=f32,
            )
            peak = jnp.max(scores, axis=0, keepdims=True) * scale
            exponent = jnp.exp2(scores * scale - peak)
            total = jnp.sum(exponent, axis=0, keepdims=True)
            weighted = lax.dot_general(
                v_buf[h, pl.ds(t, tile), :],
                exponent.astype(bf16),
                (((0,), (0,)), ((), ())),
                preferred_element_type=f32,
            )
            partials.append((peak, total, weighted))
        peak, total, weighted = merge(partials)
        mine_weighted[...] = weighted
        mine_stat[0:1, :] = peak
        mine_stat[1:2, :] = total

        def mine():
            return mine_stat[0:1, :], mine_stat[1:2, :], mine_weighted[...]

        @pl.when((step < chips) if owners == 1 else (step >= 0))
        def _():
            put(core_out, chip, mine())
            start(to_core(chip))

        @pl.when((step >= chips) if owners == 1 else (step >= 0))
        def _():
            for copy in to_core(chip):
                copy.wait_recv()
            two = merge([mine(), get(core_got, chip)])

            @pl.when(rank < depth)
            def _():
                put(cross_out, its_z, two)
                start(to_across(its_z))

            @pl.when(rank >= depth)
            def _():
                for copy in to_across(its_z):
                    copy.wait_recv()
                put(deep_out, its_z, merge([two, get(cross_got, its_z)]))

                @pl.when(its_z != z)
                def _():
                    start(to_z(its_z, z))

    deep_got[0][z] = deep_out[0][z]
    deep_got[1][z] = deep_out[1][z]

    @pl.loop(1, depth)
    def _(step):
        for copy in to_z(z, lax.rem(z + step, depth)):
            copy.wait_recv()

    _, total, weighted = merge([get(deep_got, i) for i in range(depth)])
    attended = (weighted / total).astype(bf16)

    folds = y_out.shape[3] // (depth * own_units)
    tall = own_units * folds
    out_rows = n * tall
    row = lax.broadcasted_iota(jnp.int32, (out_rows, rows), 0)
    column = lax.broadcasted_iota(jnp.int32, (out_rows, rows), 1)
    block = lax.div(row, tall)
    owner = device(
        lax.rem(block, depth), lax.rem(lax.div(block, depth), 2), lax.div(block, 2 * depth)
    )
    first = lax.rem(me, owners) * own_heads
    blocks = []
    for g in range(own_heads):
        place = owner * own_rows + (first + g) * own_units + lax.rem(row, own_units)
        pick = jnp.where(column == place, 1.0, 0.0).astype(bf16)
        blocks.append(
            lax.dot_general(
                pick, attended, (((1,), (1,)), ((), ())), preferred_element_type=f32
            ).astype(bf16)
        )
    own_block = jnp.concatenate(blocks, axis=1) if own_heads > 1 else blocks[0]

    w_copy.wait()

    def core_copy(c):
        return pltpu.make_async_remote_copy(
            src_ref=y_out.at[c, 1 - core],
            dst_ref=core_in.at[c],
            send_sem=y_send.at[0, c],
            recv_sem=y_recv.at[0, c],
            device_id={"ctx": sibling},
            device_id_type=MESH,
        )

    def across_copy(c):
        return pltpu.make_async_remote_copy(
            src_ref=across_out.at[c],
            dst_ref=across_in.at[c],
            send_sem=y_send.at[1, c],
            recv_sem=y_recv.at[1, c],
            device_id={"ctx": across},
            device_id_type=MESH,
        )

    def z_copy(c, target, source):
        return pltpu.make_async_remote_copy(
            src_ref=z_out.at[c, target],
            dst_ref=z_in.at[c, source],
            send_sem=z_send.at[c, target],
            recv_sem=z_recv.at[c, source],
            device_id={"ctx": device(target, y, core)},
            device_id_type=MESH,
        )

    chunks = y_out.shape[0]
    cols = y_out.shape[-1]
    stretch = width // folds
    fold = lax.rem(
        lax.div(lax.broadcasted_iota(jnp.int32, (out_rows, cols), 0), own_units), folds
    )
    for c in range(chunks):
        product = None
        for part in range(folds):
            at_part = part * stretch + c * cols
            term = jnp.dot(
                own_block, w_buf[:, at_part : at_part + cols], preferred_element_type=f32
            )
            product = term if product is None else jnp.where(fold == part, term, product)
        y_out[c] = product.astype(bf16).reshape(2, 2, depth * tall, cols)
        core_copy(c).start()
    for c in range(chunks):
        core_copy(c).wait_recv()
        across_out[c] = (
            y_out[c, core, 1 - y].astype(f32) + core_in[c, 1 - y].astype(f32)
        ).astype(bf16)
        across_copy(c).start()
    for c in range(chunks):
        own_sum = y_out[c, core, y].astype(f32) + core_in[c, y].astype(f32)
        across_copy(c).wait_recv()
        own_sum = (own_sum + across_in[c].astype(f32)).reshape(depth, tall, cols)
        z_out[c] = own_sum.astype(bf16)

        @pl.loop(1, depth)
        def _(step):
            z_copy(c, lax.rem(z + step, depth), z).start()

        z_in[c, z] = z_out[c, z]
    branches = []
    for c in range(chunks):

        @pl.loop(1, depth)
        def _(step):
            z_copy(c, z, lax.rem(z + step, depth)).wait_recv()

        branches.append(jnp.sum(z_in[c].astype(f32), axis=0))
    squares = sum(jnp.sum(b * b, axis=1, keepdims=True) for b in branches)
    squares = sum(squares[p * own_units : (p + 1) * own_units] for p in range(folds))
    inverse = lax.rsqrt(squares / width + 1e-06)
    for c, branch in enumerate(branches):
        for p in range(folds):
            span = pl.ds(p * stretch + c * cols, cols)
            gain = gain_ref[span].reshape(1, cols)
            mine = branch[p * own_units : (p + 1) * own_units]
            out_ref[:, span] = res_ref[:, span].astype(f32) + mine * inverse * gain

    @pl.loop(0, n)
    def _(step):
        @pl.when(step != 2 * depth)
        def _():
            q_copy(me, sibling, step).wait_send()

    @pl.loop(0, chips)
    def _(chip):
        for copy in to_core(chip):
            copy.wait_send()

    @pl.loop(0, depth)
    def _(its_z):
        for copy in to_across(its_z):
            copy.wait_send()

        @pl.when(its_z != z)
        def _():
            for copy in to_z(its_z, z):
                copy.wait_send()

    for c in range(chunks):
        core_copy(c).wait_send()
        across_copy(c).wait_send()

        @pl.loop(1, depth)
        def _(step):
            z_copy(c, lax.rem(z + step, depth), z).wait_send()


def shards(n, queries, keys, values, residual, post_gain, out_weight):
    kv_heads, context, head_dim = keys.shape
    own_units, all_width = queries.shape
    head_count = all_width // head_dim
    group_size = head_count // kv_heads
    own_rows = own_units * group_size
    rows = n * own_rows
    width = residual.shape[1]
    folds = max(1, 8 // own_units)
    tall = own_units * folds
    cols = chunk_of(width // folds, 1024)
    chunks = width // folds // cols
    depth = n // 4
    vmem = pl.BlockSpec(memory_space=pltpu.VMEM)
    hbm = pl.BlockSpec(memory_space=pl.ANY)
    dma = pltpu.SemaphoreType.DMA

    def partials(count):
        return [
            pltpu.VMEM((count, head_dim, rows), bf16),
            pltpu.VMEM((count, 8, rows), f32),
        ]

    return pl.pallas_call(
        functools.partial(kernel, n, group_size),
        out_shape=jax.ShapeDtypeStruct((own_units, width), f32),
        in_specs=[vmem, hbm, hbm, vmem, vmem, hbm],
        out_specs=vmem,
        scratch_shapes=[
            pltpu.VMEM(keys.shape, bf16),
            pltpu.VMEM(values.shape, bf16),
            pltpu.VMEM(out_weight.shape, bf16),
            pltpu.VMEM((n, kv_heads, own_rows, head_dim), bf16),
            partials(n // 2),
            partials(n // 2),
            partials(depth),
            partials(depth),
            partials(depth),
            partials(depth),
            pltpu.VMEM((head_dim, rows), f32),
            pltpu.VMEM((8, rows), f32),
            pltpu.VMEM((chunks, 2, 2, depth * tall, cols), bf16),
            pltpu.VMEM((chunks, 2, depth * tall, cols), bf16),
            pltpu.VMEM((chunks, depth * tall, cols), bf16),
            pltpu.VMEM((chunks, depth * tall, cols), bf16),
            pltpu.VMEM((chunks, depth, tall, cols), bf16),
            pltpu.VMEM((chunks, depth, tall, cols), bf16),
            dma((kv_heads,)),
            dma((kv_heads,)),
            dma,
            dma((n,)),
            dma((n,)),
            dma((3, 2, n // 2)),
            dma((3, 2, n // 2)),
            dma((2, chunks)),
            dma((2, chunks)),
            dma((chunks, depth)),
            dma((chunks, depth)),
        ],
        compiler_params=pltpu.CompilerParams(
            collective_id=0, has_side_effects=True, vmem_limit_bytes=56 * 2**20
        ),
        cost_estimate=pl.CostEstimate(
            flops=4 * kv_heads * context * rows * head_dim,
            bytes_accessed=4 * kv_heads * context * head_dim,
            transcendentals=kv_heads * context * rows,
        ),
    )(queries, keys, values, residual, post_gain, out_weight)


def solution(mesh):
    in_specs = (
        P(("groups", "ctx"), None),
        P(None, ("groups", "ctx"), None),
        P(None, ("groups", "ctx"), None),
        P(("groups", "ctx"), None),
        P(),
        P("ctx", None),
    )
    out_specs = P(("groups", "ctx"), None)
    return jax.shard_map(
        functools.partial(shards, mesh.shape["ctx"]),
        mesh=mesh,
        in_specs=in_specs,
        out_specs=out_specs,
        check_vma=False,
    )
```

```python
import functools

import jax
import jax.numpy as jnp
from jax import lax
from jax.experimental import pallas as pl
from jax.experimental.pallas import tpu as pltpu
from jax.sharding import PartitionSpec as P

MESH = pl.DeviceIdType.MESH
f32, bf16 = jnp.float32, jnp.bfloat16


def chunk_of(extent, largest):
    return max(c for c in range(128, largest + 1, 128) if extent % c == 0)


def kernel(
    n,
    group_size,
    q_ref,
    k_hbm,
    v_hbm,
    res_ref,
    gain_ref,
    w_hbm,
    out_ref,
    k_buf,
    v_buf,
    w_buf,
    q_all,
    core_out,
    core_got,
    cross_out,
    cross_got,
    deep_out,
    deep_got,
    mine_weighted,
    mine_stat,
    y_out,
    core_in,
    across_out,
    across_in,
    z_out,
    z_in,
    k_sem,
    v_sem,
    w_sem,
    q_send,
    q_recv,
    p_send,
    p_recv,
    y_send,
    y_recv,
    z_send,
    z_recv,
):
    me = lax.axis_index("ctx")
    core = lax.rem(me, 2)
    sibling = me + 1 - 2 * core
    depth = n // 4
    y = lax.rem(lax.div(me, 2), 2)
    z = lax.div(me, 4)

    def device(its_z, its_y, its_core):
        return (its_z * 2 + its_y) * 2 + its_core

    across = device(z, 1 - y, core)
    kv_heads, context, head_dim = k_buf.shape
    own_units = q_ref.shape[0]
    owners = n // kv_heads
    own_heads = group_size // owners
    own_rows = own_units * group_size
    rows = n * own_rows
    units = n * own_units
    width = w_buf.shape[1]
    scale = 168.0**-0.5
    chips = n // 2

    def place_at(rank):
        its_y = jnp.where(rank < depth, 1 - y, y)
        return lax.rem(z + 1 + rank, depth), its_y

    def head_at(step):
        rank = lax.rem(step, chips)
        its_z, its_y = place_at(rank)
        chip = its_z * 2 + its_y
        if owners > 1:
            return chip
        return chip * 2 + jnp.where(step < chips, 1 - core, core)

    def k_copy(h):
        return pltpu.make_async_copy(k_hbm.at[h], k_buf.at[h], k_sem.at[h])

    def v_copy(h):
        return pltpu.make_async_copy(v_hbm.at[h], v_buf.at[h], v_sem.at[h])

    w_copy = pltpu.make_async_copy(w_hbm, w_buf, w_sem)

    def load(step):
        k_copy(head_at(step)).start()
        v_copy(head_at(step)).start()

    first_loads = min(3, kv_heads)
    ahead = min(first_loads + 3, kv_heads)

    @pl.loop(0, first_loads)
    def _(step):
        load(step)

    barrier = pltpu.get_barrier_semaphore()

    def greet(target):
        pl.semaphore_signal(barrier, inc=1, device_id={"ctx": target}, device_id_type=MESH)

    greet(sibling)
    greet(across)

    @pl.loop(1, depth)
    def _(step):
        greet(device(lax.rem(z + step, depth), y, core))

    own = q_ref[...].astype(f32)
    for h in range(kv_heads):
        first = h * group_size * head_dim
        q_all[me, h] = jnp.concatenate(
            [own[:, first + g * head_dim :][:, :head_dim] for g in range(group_size)], axis=0
        ).astype(bf16)

    pl.semaphore_wait(barrier, depth + 1)

    def q_copy(block, target, slot):
        return pltpu.make_async_remote_copy(
            src_ref=q_all.at[block],
            dst_ref=q_all.at[block],
            send_sem=q_send.at[slot],
            recv_sem=q_recv.at[block],
            device_id={"ctx": target},
            device_id_type=MESH,
        )

    def at_z(step, its_y):
        return device(lax.rem(z + step, depth), its_y, core)

    @pl.loop(1, depth)
    def _(step):
        q_copy(me, at_z(step, y), step).start()

    q_copy(me, across, 0).start()
    q_copy(me, sibling, depth).start()

    @pl.loop(first_loads, ahead)
    def _(step):
        load(step)

    @pl.loop(1, depth)
    def _(step):
        source = at_z(depth - step, y)
        q_copy(source, sibling, 0).wait_recv()
        q_copy(source, across, 2 * depth + step).start()
        q_copy(source, sibling, depth + step).start()

    @pl.loop(0, depth)
    def _(step):
        source = at_z(depth - step, 1 - y)
        q_copy(source, sibling, 0).wait_recv()
        q_copy(source, sibling, 3 * depth + step).start()

    @pl.loop(0, n // 2)
    def _(step):
        q_copy(2 * step + 1 - core, sibling, 0).wait_recv()

    def part_copies(target, out, into, kind, slot, landing):
        return [
            pltpu.make_async_remote_copy(
                src_ref=source,
                dst_ref=destination,
                send_sem=p_send.at[kind, i, slot],
                recv_sem=p_recv.at[kind, i, landing],
                device_id={"ctx": target},
                device_id_type=MESH,
            )
            for i, (source, destination) in enumerate(zip(out, into))
        ]

    def at(refs, i):
        return [ref.at[i] for ref in refs]

    def to_core(chip):
        return part_copies(sibling, at(core_out, chip), at(core_got, chip), 0, chip, chip)

    def to_across(its_z):
        return part_copies(across, at(cross_out, its_z), at(cross_got, its_z), 1, its_z, its_z)

    def to_z(target, source):
        return part_copies(
            device(target, y, core), at(deep_out, target), at(deep_got, source), 2, target, source
        )

    def start(copies):
        for copy in copies:
            copy.start()

    def put(refs, i, partial):
        peak, total, weighted = partial
        row = lax.broadcasted_iota(jnp.int32, (8, rows), 0)
        refs[0][i] = weighted.astype(bf16)
        refs[1][i] = jnp.where(row == 0, peak, total)

    def get(refs, i):
        return refs[1][i, 0:1, :], refs[1][i, 1:2, :], refs[0][i].astype(f32)

    def merge(partials):
        peak = functools.reduce(jnp.maximum, [p for p, _, _ in partials])
        factors = [jnp.exp(p - peak) for p, _, _ in partials]
        total = sum(f * t for f, (_, t, _) in zip(factors, partials))
        return peak, total, sum(f * w for f, (_, _, w) in zip(factors, partials))

    tile = chunk_of(context, 512)

    @pl.loop(0, kv_heads)
    def _(step):
        @pl.when(step + ahead < kv_heads)
        def _():
            load(step + ahead)

        @pl.when(step == kv_heads // 2)
        def _():
            w_copy.start()

        h = head_at(step)
        rank = lax.rem(step, chips)
        its_z, its_y = place_at(rank)
        chip = its_z * 2 + its_y
        q = q_all[:, h].astype(f32).reshape(rows, head_dim).astype(bf16)
        k_copy(h).wait()
        v_copy(h).wait()
        partials = []
        for t in range(0, context, tile):
            scores = lax.dot_general(
                k_buf[h, pl.ds(t, tile), :],
                q,
                (((1,), (1,)), ((), ())),
                preferred_element_type=f32,
            )
            peak = jnp.max(scores, axis=0, keepdims=True) * scale
            exponent = jnp.exp(scores * scale - peak)
            total = jnp.sum(exponent, axis=0, keepdims=True)
            weighted = lax.dot_general(
                v_buf[h, pl.ds(t, tile), :],
                exponent.astype(bf16),
                (((0,), (0,)), ((), ())),
                preferred_element_type=f32,
            )
            partials.append((peak, total, weighted))
        peak, total, weighted = merge(partials)
        mine_weighted[...] = weighted
        mine_stat[0:1, :] = peak
        mine_stat[1:2, :] = total

        def mine():
            return mine_stat[0:1, :], mine_stat[1:2, :], mine_weighted[...]

        @pl.when((step < chips) if owners == 1 else (step >= 0))
        def _():
            put(core_out, chip, mine())
            start(to_core(chip))

        @pl.when((step >= chips) if owners == 1 else (step >= 0))
        def _():
            for copy in to_core(chip):
                copy.wait_recv()
            two = merge([mine(), get(core_got, chip)])

            @pl.when(rank < depth)
            def _():
                put(cross_out, its_z, two)
                start(to_across(its_z))

            @pl.when(rank >= depth)
            def _():
                for copy in to_across(its_z):
                    copy.wait_recv()
                put(deep_out, its_z, merge([two, get(cross_got, its_z)]))

                @pl.when(its_z != z)
                def _():
                    start(to_z(its_z, z))

    deep_got[0][z] = deep_out[0][z]
    deep_got[1][z] = deep_out[1][z]

    @pl.loop(1, depth)
    def _(step):
        for copy in to_z(z, lax.rem(z + step, depth)):
            copy.wait_recv()

    _, total, weighted = merge([get(deep_got, i) for i in range(depth)])
    attended = (weighted / total).astype(bf16)

    unit = lax.broadcasted_iota(jnp.int32, (units, rows), 0)
    column = lax.broadcasted_iota(jnp.int32, (units, rows), 1)
    first = lax.rem(me, owners) * own_heads
    blocks = []
    for g in range(own_heads):
        place = (
            lax.div(unit, own_units) * own_rows + (first + g) * own_units + lax.rem(unit, own_units)
        )
        pick = jnp.where(column == place, 1.0, 0.0).astype(bf16)
        blocks.append(
            lax.dot_general(
                pick, attended, (((1,), (1,)), ((), ())), preferred_element_type=f32
            ).astype(bf16)
        )
    own_block = jnp.concatenate(blocks, axis=1) if own_heads > 1 else blocks[0]

    w_copy.wait()

    def core_copy(c):
        return pltpu.make_async_remote_copy(
            src_ref=y_out.at[c, 1 - core],
            dst_ref=core_in.at[c],
            send_sem=y_send.at[0, c],
            recv_sem=y_recv.at[0, c],
            device_id={"ctx": sibling},
            device_id_type=MESH,
        )

    def across_copy(c):
        return pltpu.make_async_remote_copy(
            src_ref=across_out.at[c],
            dst_ref=across_in.at[c],
            send_sem=y_send.at[1, c],
            recv_sem=y_recv.at[1, c],
            device_id={"ctx": across},
            device_id_type=MESH,
        )

    def z_copy(c, target, source):
        return pltpu.make_async_remote_copy(
            src_ref=z_out.at[c, target],
            dst_ref=z_in.at[c, source],
            send_sem=z_send.at[c, target],
            recv_sem=z_recv.at[c, source],
            device_id={"ctx": device(target, y, core)},
            device_id_type=MESH,
        )

    chunks = y_out.shape[0]
    cols = y_out.shape[-1]
    for c in range(chunks):
        product = jnp.dot(
            own_block, w_buf[:, c * cols : (c + 1) * cols], preferred_element_type=f32
        )
        for k in range(n):
            y_out[c, k % 2, k // 2 % 2, k // 4] = product[
                k * own_units : (k + 1) * own_units
            ].astype(bf16)
        core_copy(c).start()
    for c in range(chunks):
        core_copy(c).wait_recv()
        across_out[c] = (
            y_out[c, core, 1 - y].astype(f32) + core_in[c, 1 - y].astype(f32)
        ).astype(bf16)
        across_copy(c).start()
    for c in range(chunks):
        own_sum = y_out[c, core, y].astype(f32) + core_in[c, y].astype(f32)
        across_copy(c).wait_recv()
        z_out[c] = (own_sum + across_in[c].astype(f32)).astype(bf16)

        @pl.loop(1, depth)
        def _(step):
            z_copy(c, lax.rem(z + step, depth), z).start()

        z_in[c, z] = z_out[c, z]
    branches = []
    for c in range(chunks):

        @pl.loop(1, depth)
        def _(step):
            z_copy(c, z, lax.rem(z + step, depth)).wait_recv()

        branches.append(jnp.sum(z_in[c].astype(f32), axis=0))
    squares = sum(jnp.sum(b * b, axis=1, keepdims=True) for b in branches)
    inverse = lax.rsqrt(squares / width + 1e-06)
    for c, branch in enumerate(branches):
        span = pl.ds(c * cols, cols)
        gain = gain_ref[span].reshape(1, cols)
        out_ref[:, span] = res_ref[:, span].astype(f32) + branch * inverse * gain

    @pl.loop(0, n)
    def _(step):
        @pl.when(step != 2 * depth)
        def _():
            q_copy(me, sibling, step).wait_send()

    @pl.loop(0, chips)
    def _(chip):
        for copy in to_core(chip):
            copy.wait_send()

    @pl.loop(0, depth)
    def _(its_z):
        for copy in to_across(its_z):
            copy.wait_send()

        @pl.when(its_z != z)
        def _():
            for copy in to_z(its_z, z):
                copy.wait_send()

    for c in range(chunks):
        core_copy(c).wait_send()
        across_copy(c).wait_send()

        @pl.loop(1, depth)
        def _(step):
            z_copy(c, lax.rem(z + step, depth), z).wait_send()


def shards(n, queries, keys, values, residual, post_gain, out_weight):
    kv_heads, context, head_dim = keys.shape
    own_units, all_width = queries.shape
    head_count = all_width // head_dim
    group_size = head_count // kv_heads
    own_rows = own_units * group_size
    rows = n * own_rows
    width = residual.shape[1]
    cols = chunk_of(width, 2048)
    chunks = width // cols
    depth = n // 4
    vmem = pl.BlockSpec(memory_space=pltpu.VMEM)
    hbm = pl.BlockSpec(memory_space=pl.ANY)
    dma = pltpu.SemaphoreType.DMA

    def partials(count):
        return [
            pltpu.VMEM((count, head_dim, rows), bf16),
            pltpu.VMEM((count, 8, rows), f32),
        ]

    return pl.pallas_call(
        functools.partial(kernel, n, group_size),
        out_shape=jax.ShapeDtypeStruct((own_units, width), f32),
        in_specs=[vmem, hbm, hbm, vmem, vmem, hbm],
        out_specs=vmem,
        scratch_shapes=[
            pltpu.VMEM(keys.shape, bf16),
            pltpu.VMEM(values.shape, bf16),
            pltpu.VMEM(out_weight.shape, bf16),
            pltpu.VMEM((n, kv_heads, own_rows, head_dim), bf16),
            partials(n // 2),
            partials(n // 2),
            partials(depth),
            partials(depth),
            partials(depth),
            partials(depth),
            pltpu.VMEM((head_dim, rows), f32),
            pltpu.VMEM((8, rows), f32),
            pltpu.VMEM((chunks, 2, 2, depth, own_units, cols), bf16),
            pltpu.VMEM((chunks, 2, depth, own_units, cols), bf16),
            pltpu.VMEM((chunks, depth, own_units, cols), bf16),
            pltpu.VMEM((chunks, depth, own_units, cols), bf16),
            pltpu.VMEM((chunks, depth, own_units, cols), bf16),
            pltpu.VMEM((chunks, depth, own_units, cols), bf16),
            dma((kv_heads,)),
            dma((kv_heads,)),
            dma,
            dma((n,)),
            dma((n,)),
            dma((3, 2, n // 2)),
            dma((3, 2, n // 2)),
            dma((2, chunks)),
            dma((2, chunks)),
            dma((chunks, depth)),
            dma((chunks, depth)),
        ],
        compiler_params=pltpu.CompilerParams(
            collective_id=0, has_side_effects=True, vmem_limit_bytes=56 * 2**20
        ),
        cost_estimate=pl.CostEstimate(
            flops=4 * kv_heads * context * rows * head_dim,
            bytes_accessed=4 * kv_heads * context * head_dim,
            transcendentals=kv_heads * context * rows,
        ),
    )(queries, keys, values, residual, post_gain, out_weight)


def solution(mesh):
    in_specs = (
        P(("groups", "ctx"), None),
        P(None, ("groups", "ctx"), None),
        P(None, ("groups", "ctx"), None),
        P(("groups", "ctx"), None),
        P(),
        P("ctx", None),
    )
    out_specs = P(("groups", "ctx"), None)
    return jax.shard_map(
        functools.partial(shards, mesh.shape["ctx"]),
        mesh=mesh,
        in_specs=in_specs,
        out_specs=out_specs,
        check_vma=False,
    )
```

```python
import functools
import math

import jax
import jax.numpy as jnp
from jax import lax
from jax.experimental import pallas as pl
from jax.experimental.pallas import tpu as pltpu
from jax.sharding import PartitionSpec as P

MESH = pl.DeviceIdType.MESH
f32, bf16 = jnp.float32, jnp.bfloat16


def chunk_of(extent, largest):
    return max(c for c in range(128, largest + 1, 128) if extent % c == 0)


def kernel(
    n,
    group_size,
    q_ref,
    k_hbm,
    v_hbm,
    res_ref,
    gain_ref,
    w_hbm,
    out_ref,
    k_buf,
    v_buf,
    w_buf,
    q_all,
    core_out,
    core_got,
    cross_out,
    cross_got,
    deep_out,
    deep_got,
    mine_weighted,
    mine_stat,
    y_out,
    core_in,
    across_out,
    across_in,
    z_out,
    z_in,
    k_sem,
    v_sem,
    w_sem,
    q_send,
    q_recv,
    p_send,
    p_recv,
    y_send,
    y_recv,
    z_send,
    z_recv,
):
    me = lax.axis_index("ctx")
    core = lax.rem(me, 2)
    sibling = me + 1 - 2 * core
    depth = n // 4
    y = lax.rem(lax.div(me, 2), 2)
    z = lax.div(me, 4)

    def device(its_z, its_y, its_core):
        return (its_z * 2 + its_y) * 2 + its_core

    across = device(z, 1 - y, core)
    kv_heads, context, head_dim = k_buf.shape
    own_units = q_ref.shape[0]
    owners = n // kv_heads
    own_heads = group_size // owners
    own_rows = own_units * group_size
    rows = n * own_rows
    units = n * own_units
    width = w_buf.shape[1]
    scale = 168.0**-0.5 * math.log2(math.e)
    chips = n // 2

    def place_at(rank):
        its_y = jnp.where(rank < depth, 1 - y, y)
        return lax.rem(z + 1 + rank, depth), its_y

    def head_at(step):
        rank = lax.rem(step, chips)
        its_z, its_y = place_at(rank)
        chip = its_z * 2 + its_y
        if owners > 1:
            return chip
        return chip * 2 + jnp.where(step < chips, 1 - core, core)

    def k_copy(h):
        return pltpu.make_async_copy(k_hbm.at[h], k_buf.at[h], k_sem.at[h])

    def v_copy(h):
        return pltpu.make_async_copy(v_hbm.at[h], v_buf.at[h], v_sem.at[h])

    w_copy = pltpu.make_async_copy(w_hbm, w_buf, w_sem)

    def load(step):
        k_copy(head_at(step)).start()
        v_copy(head_at(step)).start()

    first_loads = min(3, kv_heads)
    ahead = min(first_loads + 3, kv_heads)

    @pl.loop(0, first_loads)
    def _(step):
        load(step)

    barrier = pltpu.get_barrier_semaphore()

    def greet(target):
        pl.semaphore_signal(barrier, inc=1, device_id={"ctx": target}, device_id_type=MESH)

    greet(sibling)
    greet(across)

    @pl.loop(1, depth)
    def _(step):
        greet(device(lax.rem(z + step, depth), y, core))

    own = q_ref[...].astype(f32)
    for h in range(kv_heads):
        first = h * group_size * head_dim
        q_all[me, h] = jnp.concatenate(
            [own[:, first + g * head_dim :][:, :head_dim] for g in range(group_size)], axis=0
        ).astype(bf16)

    pl.semaphore_wait(barrier, depth + 1)

    def q_copy(block, target, slot):
        return pltpu.make_async_remote_copy(
            src_ref=q_all.at[block],
            dst_ref=q_all.at[block],
            send_sem=q_send.at[slot],
            recv_sem=q_recv.at[block],
            device_id={"ctx": target},
            device_id_type=MESH,
        )

    def at_z(step, its_y):
        return device(lax.rem(z + step, depth), its_y, core)

    @pl.loop(1, depth)
    def _(step):
        q_copy(me, at_z(step, y), step).start()

    q_copy(me, across, 0).start()
    q_copy(me, sibling, depth).start()

    @pl.loop(first_loads, ahead)
    def _(step):
        load(step)

    @pl.loop(1, depth)
    def _(step):
        source = at_z(depth - step, y)
        q_copy(source, sibling, 0).wait_recv()
        q_copy(source, across, 2 * depth + step).start()
        q_copy(source, sibling, depth + step).start()

    @pl.loop(0, depth)
    def _(step):
        source = at_z(depth - step, 1 - y)
        q_copy(source, sibling, 0).wait_recv()
        q_copy(source, sibling, 3 * depth + step).start()

    @pl.loop(0, n // 2)
    def _(step):
        q_copy(2 * step + 1 - core, sibling, 0).wait_recv()

    def part_copies(target, out, into, kind, slot, landing):
        return [
            pltpu.make_async_remote_copy(
                src_ref=source,
                dst_ref=destination,
                send_sem=p_send.at[kind, i, slot],
                recv_sem=p_recv.at[kind, i, landing],
                device_id={"ctx": target},
                device_id_type=MESH,
            )
            for i, (source, destination) in enumerate(zip(out, into))
        ]

    def at(refs, i):
        return [ref.at[i] for ref in refs]

    def to_core(chip):
        return part_copies(sibling, at(core_out, chip), at(core_got, chip), 0, chip, chip)

    def to_across(its_z):
        return part_copies(across, at(cross_out, its_z), at(cross_got, its_z), 1, its_z, its_z)

    def to_z(target, source):
        return part_copies(
            device(target, y, core), at(deep_out, target), at(deep_got, source), 2, target, source
        )

    def start(copies):
        for copy in copies:
            copy.start()

    def put(refs, i, partial):
        peak, total, weighted = partial
        row = lax.broadcasted_iota(jnp.int32, (8, rows), 0)
        refs[0][i] = weighted.astype(bf16)
        refs[1][i] = jnp.where(row == 0, peak, total)

    def get(refs, i):
        return refs[1][i, 0:1, :], refs[1][i, 1:2, :], refs[0][i].astype(f32)

    def merge(partials):
        peak = functools.reduce(jnp.maximum, [p for p, _, _ in partials])
        factors = [jnp.exp2(p - peak) for p, _, _ in partials]
        total = sum(f * t for f, (_, t, _) in zip(factors, partials))
        return peak, total, sum(f * w for f, (_, _, w) in zip(factors, partials))

    tile = chunk_of(context, 512)

    def exchange(i, step):
        rank = lax.rem(step, chips)
        its_z, its_y = place_at(rank)
        chip = its_z * 2 + its_y

        def mine():
            return mine_stat[i, 0:1, :], mine_stat[i, 1:2, :], mine_weighted[i]

        @pl.when((step < chips) if owners == 1 else (step >= 0))
        def _():
            put(core_out, chip, mine())
            start(to_core(chip))

        @pl.when((step >= chips) if owners == 1 else (step >= 0))
        def _():
            for copy in to_core(chip):
                copy.wait_recv()
            two = merge([mine(), get(core_got, chip)])

            @pl.when(rank < depth)
            def _():
                put(cross_out, its_z, two)
                start(to_across(its_z))

            @pl.when(rank >= depth)
            def _():
                for copy in to_across(its_z):
                    copy.wait_recv()
                put(deep_out, its_z, merge([two, get(cross_got, its_z)]))

                @pl.when(its_z != z)
                def _():
                    start(to_z(its_z, z))

    @pl.loop(0, kv_heads // 2)
    def _(pair):
        steps = [2 * pair, 2 * pair + 1]
        heads = [head_at(step) for step in steps]
        for step in steps:

            @pl.when(step + ahead < kv_heads)
            def _():
                load(step + ahead)

        @pl.when(pair == kv_heads // 4)
        def _():
            w_copy.start()

        empty = jnp.zeros((rows, head_dim), bf16)
        q0, q1 = [q_all[:, h].astype(f32).reshape(rows, head_dim).astype(bf16) for h in heads]
        q = jnp.concatenate(
            [jnp.concatenate([q0, empty], axis=1), jnp.concatenate([empty, q1], axis=1)], axis=0
        )
        for h in heads:
            k_copy(h).wait()
            v_copy(h).wait()
        partials = [[], []]
        for t in range(0, context, tile):
            span = pl.ds(t, tile)
            scores = lax.dot_general(
                jnp.concatenate([k_buf[h, span, :] for h in heads], axis=1),
                q,
                (((1,), (1,)), ((), ())),
                preferred_element_type=f32,
            )
            peak = jnp.max(scores, axis=0, keepdims=True) * scale
            exponent = jnp.exp2(scores * scale - peak)
            total = jnp.sum(exponent, axis=0, keepdims=True)
            weights = exponent.astype(bf16)
            for i, h in enumerate(heads):
                half = slice(i * rows, (i + 1) * rows)
                weighted = lax.dot_general(
                    v_buf[h, span, :],
                    weights[:, half],
                    (((0,), (0,)), ((), ())),
                    preferred_element_type=f32,
                )
                partials[i].append((peak[:, half], total[:, half], weighted))
        for i in range(2):
            peak, total, weighted = merge(partials[i])
            mine_weighted[i] = weighted
            mine_stat[i, 0:1, :] = peak
            mine_stat[i, 1:2, :] = total
        for i, step in enumerate(steps):
            exchange(i, step)

    deep_got[0][z] = deep_out[0][z]
    deep_got[1][z] = deep_out[1][z]

    @pl.loop(1, depth)
    def _(step):
        for copy in to_z(z, lax.rem(z + step, depth)):
            copy.wait_recv()

    _, total, weighted = merge([get(deep_got, i) for i in range(depth)])
    attended = (weighted / total).astype(bf16)

    unit = lax.broadcasted_iota(jnp.int32, (units, rows), 0)
    column = lax.broadcasted_iota(jnp.int32, (units, rows), 1)
    first = lax.rem(me, owners) * own_heads
    blocks = []
    for g in range(own_heads):
        place = (
            lax.div(unit, own_units) * own_rows + (first + g) * own_units + lax.rem(unit, own_units)
        )
        pick = jnp.where(column == place, 1.0, 0.0).astype(bf16)
        blocks.append(
            lax.dot_general(
                pick, attended, (((1,), (1,)), ((), ())), preferred_element_type=f32
            ).astype(bf16)
        )
    own_block = jnp.concatenate(blocks, axis=1) if own_heads > 1 else blocks[0]

    w_copy.wait()

    def core_copy(c):
        return pltpu.make_async_remote_copy(
            src_ref=y_out.at[c, 1 - core],
            dst_ref=core_in.at[c],
            send_sem=y_send.at[0, c],
            recv_sem=y_recv.at[0, c],
            device_id={"ctx": sibling},
            device_id_type=MESH,
        )

    def across_copy(c):
        return pltpu.make_async_remote_copy(
            src_ref=across_out.at[c],
            dst_ref=across_in.at[c],
            send_sem=y_send.at[1, c],
            recv_sem=y_recv.at[1, c],
            device_id={"ctx": across},
            device_id_type=MESH,
        )

    def z_copy(c, target, source):
        return pltpu.make_async_remote_copy(
            src_ref=z_out.at[c, target],
            dst_ref=z_in.at[c, source],
            send_sem=z_send.at[c, target],
            recv_sem=z_recv.at[c, source],
            device_id={"ctx": device(target, y, core)},
            device_id_type=MESH,
        )

    chunks = y_out.shape[0]
    cols = y_out.shape[-1]
    for c in range(chunks):
        product = jnp.dot(
            own_block, w_buf[:, c * cols : (c + 1) * cols], preferred_element_type=f32
        )
        for k in range(n):
            y_out[c, k % 2, k // 2 % 2, k // 4] = product[
                k * own_units : (k + 1) * own_units
            ].astype(bf16)
        core_copy(c).start()
    for c in range(chunks):
        core_copy(c).wait_recv()
        across_out[c] = (
            y_out[c, core, 1 - y].astype(f32) + core_in[c, 1 - y].astype(f32)
        ).astype(bf16)
        across_copy(c).start()
    for c in range(chunks):
        own_sum = y_out[c, core, y].astype(f32) + core_in[c, y].astype(f32)
        across_copy(c).wait_recv()
        z_out[c] = (own_sum + across_in[c].astype(f32)).astype(bf16)

        @pl.loop(1, depth)
        def _(step):
            z_copy(c, lax.rem(z + step, depth), z).start()

        z_in[c, z] = z_out[c, z]
    branches = []
    for c in range(chunks):

        @pl.loop(1, depth)
        def _(step):
            z_copy(c, z, lax.rem(z + step, depth)).wait_recv()

        branches.append(jnp.sum(z_in[c].astype(f32), axis=0))
    squares = sum(jnp.sum(b * b, axis=1, keepdims=True) for b in branches)
    inverse = lax.rsqrt(squares / width + 1e-06)
    for c, branch in enumerate(branches):
        span = pl.ds(c * cols, cols)
        gain = gain_ref[span].reshape(1, cols)
        out_ref[:, span] = res_ref[:, span].astype(f32) + branch * inverse * gain

    @pl.loop(0, n)
    def _(step):
        @pl.when(step != 2 * depth)
        def _():
            q_copy(me, sibling, step).wait_send()

    @pl.loop(0, chips)
    def _(chip):
        for copy in to_core(chip):
            copy.wait_send()

    @pl.loop(0, depth)
    def _(its_z):
        for copy in to_across(its_z):
            copy.wait_send()

        @pl.when(its_z != z)
        def _():
            for copy in to_z(its_z, z):
                copy.wait_send()

    for c in range(chunks):
        core_copy(c).wait_send()
        across_copy(c).wait_send()

        @pl.loop(1, depth)
        def _(step):
            z_copy(c, lax.rem(z + step, depth), z).wait_send()


def shards(n, queries, keys, values, residual, post_gain, out_weight):
    kv_heads, context, head_dim = keys.shape
    own_units, all_width = queries.shape
    head_count = all_width // head_dim
    group_size = head_count // kv_heads
    own_rows = own_units * group_size
    rows = n * own_rows
    width = residual.shape[1]
    cols = chunk_of(width, 2048)
    chunks = width // cols
    depth = n // 4
    vmem = pl.BlockSpec(memory_space=pltpu.VMEM)
    hbm = pl.BlockSpec(memory_space=pl.ANY)
    dma = pltpu.SemaphoreType.DMA

    def partials(count):
        return [
            pltpu.VMEM((count, head_dim, rows), bf16),
            pltpu.VMEM((count, 8, rows), f32),
        ]

    return pl.pallas_call(
        functools.partial(kernel, n, group_size),
        out_shape=jax.ShapeDtypeStruct((own_units, width), f32),
        in_specs=[vmem, hbm, hbm, vmem, vmem, hbm],
        out_specs=vmem,
        scratch_shapes=[
            pltpu.VMEM(keys.shape, bf16),
            pltpu.VMEM(values.shape, bf16),
            pltpu.VMEM(out_weight.shape, bf16),
            pltpu.VMEM((n, kv_heads, own_rows, head_dim), bf16),
            partials(n // 2),
            partials(n // 2),
            partials(depth),
            partials(depth),
            partials(depth),
            partials(depth),
            pltpu.VMEM((2, head_dim, rows), f32),
            pltpu.VMEM((2, 8, rows), f32),
            pltpu.VMEM((chunks, 2, 2, depth, own_units, cols), bf16),
            pltpu.VMEM((chunks, 2, depth, own_units, cols), bf16),
            pltpu.VMEM((chunks, depth, own_units, cols), bf16),
            pltpu.VMEM((chunks, depth, own_units, cols), bf16),
            pltpu.VMEM((chunks, depth, own_units, cols), bf16),
            pltpu.VMEM((chunks, depth, own_units, cols), bf16),
            dma((kv_heads,)),
            dma((kv_heads,)),
            dma,
            dma((n,)),
            dma((n,)),
            dma((3, 2, n // 2)),
            dma((3, 2, n // 2)),
            dma((2, chunks)),
            dma((2, chunks)),
            dma((chunks, depth)),
            dma((chunks, depth)),
        ],
        compiler_params=pltpu.CompilerParams(
            collective_id=0, has_side_effects=True, vmem_limit_bytes=56 * 2**20
        ),
        cost_estimate=pl.CostEstimate(
            flops=4 * kv_heads * context * rows * head_dim,
            bytes_accessed=4 * kv_heads * context * head_dim,
            transcendentals=kv_heads * context * rows,
        ),
    )(queries, keys, values, residual, post_gain, out_weight)


def solution(mesh):
    in_specs = (
        P(("groups", "ctx"), None),
        P(None, ("groups", "ctx"), None),
        P(None, ("groups", "ctx"), None),
        P(("groups", "ctx"), None),
        P(),
        P("ctx", None),
    )
    out_specs = P(("groups", "ctx"), None)
    return jax.shard_map(
        functools.partial(shards, mesh.shape["ctx"]),
        mesh=mesh,
        in_specs=in_specs,
        out_specs=out_specs,
        check_vma=False,
    )
```

```python
import functools
import math

import jax
import jax.numpy as jnp
from jax import lax
from jax.experimental import pallas as pl
from jax.experimental.pallas import tpu as pltpu
from jax.sharding import PartitionSpec as P

MESH = pl.DeviceIdType.MESH
f32, bf16 = jnp.float32, jnp.bfloat16


def chunk_of(extent, largest):
    return max(c for c in range(128, largest + 1, 128) if extent % c == 0)


def kernel(
    n,
    group_size,
    q_ref,
    k_hbm,
    v_hbm,
    res_ref,
    gain_ref,
    w_hbm,
    out_ref,
    k_buf,
    v_buf,
    v_turned,
    w_buf,
    q_all,
    core_out,
    core_got,
    cross_out,
    cross_got,
    deep_out,
    deep_got,
    mine_weighted,
    mine_stat,
    y_out,
    core_in,
    across_out,
    across_in,
    z_out,
    z_in,
    k_sem,
    v_sem,
    w_sem,
    q_send,
    q_recv,
    p_send,
    p_recv,
    y_send,
    y_recv,
    z_send,
    z_recv,
):
    me = lax.axis_index("ctx")
    core = lax.rem(me, 2)
    sibling = me + 1 - 2 * core
    depth = n // 4
    y = lax.rem(lax.div(me, 2), 2)
    z = lax.div(me, 4)

    def device(its_z, its_y, its_core):
        return (its_z * 2 + its_y) * 2 + its_core

    across = device(z, 1 - y, core)
    kv_heads, context, head_dim = k_buf.shape
    own_units = q_ref.shape[0]
    owners = n // kv_heads
    own_heads = group_size // owners
    own_rows = own_units * group_size
    rows = n * own_rows
    units = n * own_units
    width = w_buf.shape[1]
    scale = 168.0**-0.5 * math.log2(math.e)
    chips = n // 2

    def place_at(rank):
        its_y = jnp.where(rank < depth, 1 - y, y)
        return lax.rem(z + 1 + rank, depth), its_y

    def head_at(step):
        rank = lax.rem(step, chips)
        its_z, its_y = place_at(rank)
        chip = its_z * 2 + its_y
        if owners > 1:
            return chip
        return chip * 2 + jnp.where(step < chips, 1 - core, core)

    def k_copy(h):
        return pltpu.make_async_copy(k_hbm.at[h], k_buf.at[h], k_sem.at[h])

    def v_copy(h):
        return pltpu.make_async_copy(v_hbm.at[h], v_buf.at[h], v_sem.at[h])

    w_copy = pltpu.make_async_copy(w_hbm, w_buf, w_sem)

    def load(step):
        k_copy(head_at(step)).start()

    ahead = min(6, kv_heads)

    @pl.loop(0, kv_heads)
    def _(step):
        v_copy(head_at(step)).start()

    def turn(begin, end):
        @pl.loop(begin, end)
        def _(step):
            h = head_at(step)
            v_copy(h).wait()
            v_turned[h] = v_buf[h].T

    barrier = pltpu.get_barrier_semaphore()

    def greet(target):
        pl.semaphore_signal(barrier, inc=1, device_id={"ctx": target}, device_id_type=MESH)

    greet(sibling)
    greet(across)

    @pl.loop(1, depth)
    def _(step):
        greet(device(lax.rem(z + step, depth), y, core))

    own = q_ref[...].astype(f32)
    for h in range(kv_heads):
        first = h * group_size * head_dim
        q_all[me, h] = jnp.concatenate(
            [own[:, first + g * head_dim :][:, :head_dim] for g in range(group_size)], axis=0
        ).astype(bf16)

    pl.semaphore_wait(barrier, depth + 1)

    def q_copy(block, target, slot):
        return pltpu.make_async_remote_copy(
            src_ref=q_all.at[block],
            dst_ref=q_all.at[block],
            send_sem=q_send.at[slot],
            recv_sem=q_recv.at[block],
            device_id={"ctx": target},
            device_id_type=MESH,
        )

    def at_z(step, its_y):
        return device(lax.rem(z + step, depth), its_y, core)

    @pl.loop(1, depth)
    def _(step):
        q_copy(me, at_z(step, y), step).start()

    q_copy(me, across, 0).start()
    q_copy(me, sibling, depth).start()

    @pl.loop(0, ahead)
    def _(step):
        load(step)

    third = kv_heads // 3
    turn(0, third)

    @pl.loop(1, depth)
    def _(step):
        source = at_z(depth - step, y)
        q_copy(source, sibling, 0).wait_recv()
        q_copy(source, across, 2 * depth + step).start()
        q_copy(source, sibling, depth + step).start()

    turn(third, 2 * third)

    @pl.loop(0, depth)
    def _(step):
        source = at_z(depth - step, 1 - y)
        q_copy(source, sibling, 0).wait_recv()
        q_copy(source, sibling, 3 * depth + step).start()

    turn(2 * third, kv_heads)

    @pl.loop(0, n // 2)
    def _(step):
        q_copy(2 * step + 1 - core, sibling, 0).wait_recv()

    def part_copies(target, out, into, kind, slot, landing):
        return [
            pltpu.make_async_remote_copy(
                src_ref=source,
                dst_ref=destination,
                send_sem=p_send.at[kind, i, slot],
                recv_sem=p_recv.at[kind, i, landing],
                device_id={"ctx": target},
                device_id_type=MESH,
            )
            for i, (source, destination) in enumerate(zip(out, into))
        ]

    def at(refs, i):
        return [ref.at[i] for ref in refs]

    def to_core(chip):
        return part_copies(sibling, at(core_out, chip), at(core_got, chip), 0, chip, chip)

    def to_across(its_z):
        return part_copies(across, at(cross_out, its_z), at(cross_got, its_z), 1, its_z, its_z)

    def to_z(target, source):
        return part_copies(
            device(target, y, core), at(deep_out, target), at(deep_got, source), 2, target, source
        )

    def start(copies):
        for copy in copies:
            copy.start()

    def put(refs, i, partial):
        peak, total, weighted = partial
        row = lax.broadcasted_iota(jnp.int32, (8, rows), 0)
        refs[0][i] = weighted.astype(bf16)
        refs[1][i] = jnp.where(row == 0, peak, total)

    def get(refs, i):
        return refs[1][i, 0:1, :], refs[1][i, 1:2, :], refs[0][i].astype(f32)

    def merge(partials):
        peak = functools.reduce(jnp.maximum, [p for p, _, _ in partials])
        factors = [jnp.exp2(p - peak) for p, _, _ in partials]
        total = sum(f * t for f, (_, t, _) in zip(factors, partials))
        return peak, total, sum(f * w for f, (_, _, w) in zip(factors, partials))

    tile = chunk_of(context, 512)

    def exchange(i, step):
        rank = lax.rem(step, chips)
        its_z, its_y = place_at(rank)
        chip = its_z * 2 + its_y

        def mine():
            return mine_stat[i, 0:1, :], mine_stat[i, 1:2, :], mine_weighted[i]

        @pl.when((step < chips) if owners == 1 else (step >= 0))
        def _():
            put(core_out, chip, mine())
            start(to_core(chip))

        @pl.when((step >= chips) if owners == 1 else (step >= 0))
        def _():
            for copy in to_core(chip):
                copy.wait_recv()
            two = merge([mine(), get(core_got, chip)])

            @pl.when(rank < depth)
            def _():
                put(cross_out, its_z, two)
                start(to_across(its_z))

            @pl.when(rank >= depth)
            def _():
                for copy in to_across(its_z):
                    copy.wait_recv()
                put(deep_out, its_z, merge([two, get(cross_got, its_z)]))

                @pl.when(its_z != z)
                def _():
                    start(to_z(its_z, z))

    @pl.loop(0, kv_heads // 2)
    def _(pair):
        steps = [2 * pair, 2 * pair + 1]
        heads = [head_at(step) for step in steps]
        for step in steps:

            @pl.when(step + ahead < kv_heads)
            def _():
                load(step + ahead)

        @pl.when(pair == kv_heads // 4)
        def _():
            w_copy.start()

        empty = jnp.zeros((rows, head_dim), bf16)
        q0, q1 = [q_all[:, h].astype(f32).reshape(rows, head_dim).astype(bf16) for h in heads]
        q = jnp.concatenate(
            [jnp.concatenate([q0, empty], axis=1), jnp.concatenate([empty, q1], axis=1)], axis=0
        )
        for h in heads:
            k_copy(h).wait()
        partials = [[], []]
        for t in range(0, context, tile):
            span = pl.ds(t, tile)
            scores = lax.dot_general(
                jnp.concatenate([k_buf[h, span, :] for h in heads], axis=1),
                q,
                (((1,), (1,)), ((), ())),
                preferred_element_type=f32,
            )
            peak = jnp.max(scores, axis=0, keepdims=True) * scale
            exponent = jnp.exp2(scores * scale - peak)
            total = jnp.sum(exponent, axis=0, keepdims=True)
            weights = exponent.astype(bf16)
            for i, h in enumerate(heads):
                half = slice(i * rows, (i + 1) * rows)
                weighted = jnp.dot(
                    v_turned[h, :, span], weights[:, half], preferred_element_type=f32
                )
                partials[i].append((peak[:, half], total[:, half], weighted))
        for i in range(2):
            peak, total, weighted = merge(partials[i])
            mine_weighted[i] = weighted
            mine_stat[i, 0:1, :] = peak
            mine_stat[i, 1:2, :] = total
        for i, step in enumerate(steps):
            exchange(i, step)

    deep_got[0][z] = deep_out[0][z]
    deep_got[1][z] = deep_out[1][z]

    @pl.loop(1, depth)
    def _(step):
        for copy in to_z(z, lax.rem(z + step, depth)):
            copy.wait_recv()

    _, total, weighted = merge([get(deep_got, i) for i in range(depth)])
    attended = (weighted / total).astype(bf16)

    unit = lax.broadcasted_iota(jnp.int32, (units, rows), 0)
    column = lax.broadcasted_iota(jnp.int32, (units, rows), 1)
    first = lax.rem(me, owners) * own_heads
    blocks = []
    for g in range(own_heads):
        place = (
            lax.div(unit, own_units) * own_rows + (first + g) * own_units + lax.rem(unit, own_units)
        )
        pick = jnp.where(column == place, 1.0, 0.0).astype(bf16)
        blocks.append(
            lax.dot_general(
                pick, attended, (((1,), (1,)), ((), ())), preferred_element_type=f32
            ).astype(bf16)
        )
    own_block = jnp.concatenate(blocks, axis=1) if own_heads > 1 else blocks[0]

    w_copy.wait()

    def core_copy(c):
        return pltpu.make_async_remote_copy(
            src_ref=y_out.at[c, 1 - core],
            dst_ref=core_in.at[c],
            send_sem=y_send.at[0, c],
            recv_sem=y_recv.at[0, c],
            device_id={"ctx": sibling},
            device_id_type=MESH,
        )

    def across_copy(c):
        return pltpu.make_async_remote_copy(
            src_ref=across_out.at[c],
            dst_ref=across_in.at[c],
            send_sem=y_send.at[1, c],
            recv_sem=y_recv.at[1, c],
            device_id={"ctx": across},
            device_id_type=MESH,
        )

    def z_copy(c, target, source):
        return pltpu.make_async_remote_copy(
            src_ref=z_out.at[c, target],
            dst_ref=z_in.at[c, source],
            send_sem=z_send.at[c, target],
            recv_sem=z_recv.at[c, source],
            device_id={"ctx": device(target, y, core)},
            device_id_type=MESH,
        )

    chunks = y_out.shape[0]
    cols = y_out.shape[-1]
    for c in range(chunks):
        product = jnp.dot(
            own_block, w_buf[:, c * cols : (c + 1) * cols], preferred_element_type=f32
        )
        for k in range(n):
            y_out[c, k % 2, k // 2 % 2, k // 4] = product[
                k * own_units : (k + 1) * own_units
            ].astype(bf16)
        core_copy(c).start()
    for c in range(chunks):
        core_copy(c).wait_recv()
        across_out[c] = (
            y_out[c, core, 1 - y].astype(f32) + core_in[c, 1 - y].astype(f32)
        ).astype(bf16)
        across_copy(c).start()
    for c in range(chunks):
        own_sum = y_out[c, core, y].astype(f32) + core_in[c, y].astype(f32)
        across_copy(c).wait_recv()
        z_out[c] = (own_sum + across_in[c].astype(f32)).astype(bf16)

        @pl.loop(1, depth)
        def _(step):
            z_copy(c, lax.rem(z + step, depth), z).start()

        z_in[c, z] = z_out[c, z]
    branches = []
    for c in range(chunks):

        @pl.loop(1, depth)
        def _(step):
            z_copy(c, z, lax.rem(z + step, depth)).wait_recv()

        branches.append(jnp.sum(z_in[c].astype(f32), axis=0))
    squares = sum(jnp.sum(b * b, axis=1, keepdims=True) for b in branches)
    inverse = lax.rsqrt(squares / width + 1e-06)
    for c, branch in enumerate(branches):
        span = pl.ds(c * cols, cols)
        gain = gain_ref[span].reshape(1, cols)
        out_ref[:, span] = res_ref[:, span].astype(f32) + branch * inverse * gain

    @pl.loop(0, n)
    def _(step):
        @pl.when(step != 2 * depth)
        def _():
            q_copy(me, sibling, step).wait_send()

    @pl.loop(0, chips)
    def _(chip):
        for copy in to_core(chip):
            copy.wait_send()

    @pl.loop(0, depth)
    def _(its_z):
        for copy in to_across(its_z):
            copy.wait_send()

        @pl.when(its_z != z)
        def _():
            for copy in to_z(its_z, z):
                copy.wait_send()

    for c in range(chunks):
        core_copy(c).wait_send()
        across_copy(c).wait_send()

        @pl.loop(1, depth)
        def _(step):
            z_copy(c, lax.rem(z + step, depth), z).wait_send()


def shards(n, queries, keys, values, residual, post_gain, out_weight):
    kv_heads, context, head_dim = keys.shape
    own_units, all_width = queries.shape
    head_count = all_width // head_dim
    group_size = head_count // kv_heads
    own_rows = own_units * group_size
    rows = n * own_rows
    width = residual.shape[1]
    cols = chunk_of(width, 2048)
    chunks = width // cols
    depth = n // 4
    vmem = pl.BlockSpec(memory_space=pltpu.VMEM)
    hbm = pl.BlockSpec(memory_space=pl.ANY)
    dma = pltpu.SemaphoreType.DMA

    def partials(count):
        return [
            pltpu.VMEM((count, head_dim, rows), bf16),
            pltpu.VMEM((count, 8, rows), f32),
        ]

    return pl.pallas_call(
        functools.partial(kernel, n, group_size),
        out_shape=jax.ShapeDtypeStruct((own_units, width), f32),
        in_specs=[vmem, hbm, hbm, vmem, vmem, hbm],
        out_specs=vmem,
        scratch_shapes=[
            pltpu.VMEM(keys.shape, bf16),
            pltpu.VMEM(values.shape, bf16),
            pltpu.VMEM((kv_heads, head_dim, context), bf16),
            pltpu.VMEM(out_weight.shape, bf16),
            pltpu.VMEM((n, kv_heads, own_rows, head_dim), bf16),
            partials(n // 2),
            partials(n // 2),
            partials(depth),
            partials(depth),
            partials(depth),
            partials(depth),
            pltpu.VMEM((2, head_dim, rows), f32),
            pltpu.VMEM((2, 8, rows), f32),
            pltpu.VMEM((chunks, 2, 2, depth, own_units, cols), bf16),
            pltpu.VMEM((chunks, 2, depth, own_units, cols), bf16),
            pltpu.VMEM((chunks, depth, own_units, cols), bf16),
            pltpu.VMEM((chunks, depth, own_units, cols), bf16),
            pltpu.VMEM((chunks, depth, own_units, cols), bf16),
            pltpu.VMEM((chunks, depth, own_units, cols), bf16),
            dma((kv_heads,)),
            dma((kv_heads,)),
            dma,
            dma((n,)),
            dma((n,)),
            dma((3, 2, n // 2)),
            dma((3, 2, n // 2)),
            dma((2, chunks)),
            dma((2, chunks)),
            dma((chunks, depth)),
            dma((chunks, depth)),
        ],
        compiler_params=pltpu.CompilerParams(
            collective_id=0, has_side_effects=True, vmem_limit_bytes=56 * 2**20
        ),
        cost_estimate=pl.CostEstimate(
            flops=4 * kv_heads * context * rows * head_dim,
            bytes_accessed=4 * kv_heads * context * head_dim,
            transcendentals=kv_heads * context * rows,
        ),
    )(queries, keys, values, residual, post_gain, out_weight)


def solution(mesh):
    in_specs = (
        P(("groups", "ctx"), None),
        P(None, ("groups", "ctx"), None),
        P(None, ("groups", "ctx"), None),
        P(("groups", "ctx"), None),
        P(),
        P("ctx", None),
    )
    out_specs = P(("groups", "ctx"), None)
    return jax.shard_map(
        functools.partial(shards, mesh.shape["ctx"]),
        mesh=mesh,
        in_specs=in_specs,
        out_specs=out_specs,
        check_vma=False,
    )
```

```python
import functools
import math

import jax
import jax.numpy as jnp
from jax import lax
from jax.experimental import pallas as pl
from jax.experimental.pallas import tpu as pltpu
from jax.sharding import PartitionSpec as P

MESH = pl.DeviceIdType.MESH
f32, bf16 = jnp.float32, jnp.bfloat16


def chunk_of(extent, largest):
    return max(c for c in range(128, largest + 1, 128) if extent % c == 0)


def kernel(
    n,
    group_size,
    q_ref,
    k_hbm,
    v_hbm,
    res_ref,
    gain_ref,
    w_hbm,
    out_ref,
    k_buf,
    v_buf,
    w_buf,
    q_all,
    core_out,
    core_got,
    cross_out,
    cross_got,
    deep_out,
    deep_got,
    mine_weighted,
    mine_stat,
    y_out,
    core_in,
    across_out,
    across_in,
    z_out,
    z_in,
    k_sem,
    v_sem,
    w_sem,
    q_send,
    q_recv,
    p_send,
    p_recv,
    y_send,
    y_recv,
    z_send,
    z_recv,
):
    me = lax.axis_index("ctx")
    core = lax.rem(me, 2)
    sibling = me + 1 - 2 * core
    depth = n // 4
    y = lax.rem(lax.div(me, 2), 2)
    z = lax.div(me, 4)

    def device(its_z, its_y, its_core):
        return (its_z * 2 + its_y) * 2 + its_core

    across = device(z, 1 - y, core)
    kv_heads, context, head_dim = k_buf.shape
    own_units = q_ref.shape[0]
    owners = n // kv_heads
    own_heads = group_size // owners
    own_rows = own_units * group_size
    rows = n * own_rows
    units = n * own_units
    width = w_buf.shape[1]
    scale = 168.0**-0.5 * math.log2(math.e)
    chips = n // 2

    def place_at(rank):
        its_y = jnp.where(rank < depth, 1 - y, y)
        return lax.rem(z + 1 + rank, depth), its_y

    def head_at(step):
        rank = lax.rem(step, chips)
        its_z, its_y = place_at(rank)
        chip = its_z * 2 + its_y
        if owners > 1:
            return chip
        return chip * 2 + jnp.where(step < chips, 1 - core, core)

    def k_copy(h):
        return pltpu.make_async_copy(k_hbm.at[h], k_buf.at[h], k_sem.at[h])

    def v_copy(h):
        return pltpu.make_async_copy(v_hbm.at[h], v_buf.at[h], v_sem.at[h])

    w_copy = pltpu.make_async_copy(w_hbm, w_buf, w_sem)

    def load(step):
        k_copy(head_at(step)).start()
        v_copy(head_at(step)).start()

    first_loads = min(3, kv_heads)
    ahead = min(first_loads + 3, kv_heads)

    @pl.loop(0, first_loads)
    def _(step):
        load(step)

    barrier = pltpu.get_barrier_semaphore()

    def greet(target):
        pl.semaphore_signal(barrier, inc=1, device_id={"ctx": target}, device_id_type=MESH)

    greet(sibling)
    greet(across)

    @pl.loop(1, depth)
    def _(step):
        greet(device(lax.rem(z + step, depth), y, core))

    own = q_ref[...].astype(f32)
    for h in range(kv_heads):
        first = h * group_size * head_dim
        q_all[me, h] = jnp.concatenate(
            [own[:, first + g * head_dim :][:, :head_dim] for g in range(group_size)], axis=0
        ).astype(bf16)

    pl.semaphore_wait(barrier, depth + 1)

    def q_copy(block, target, slot):
        return pltpu.make_async_remote_copy(
            src_ref=q_all.at[block],
            dst_ref=q_all.at[block],
            send_sem=q_send.at[slot],
            recv_sem=q_recv.at[block],
            device_id={"ctx": target},
            device_id_type=MESH,
        )

    def at_z(step, its_y):
        return device(lax.rem(z + step, depth), its_y, core)

    @pl.loop(1, depth)
    def _(step):
        q_copy(me, at_z(step, y), step).start()

    q_copy(me, across, 0).start()
    q_copy(me, sibling, depth).start()

    @pl.loop(first_loads, ahead)
    def _(step):
        load(step)

    @pl.loop(1, depth)
    def _(step):
        source = at_z(depth - step, y)
        q_copy(source, sibling, 0).wait_recv()
        q_copy(source, across, 2 * depth + step).start()
        q_copy(source, sibling, depth + step).start()

    @pl.loop(0, depth)
    def _(step):
        source = at_z(depth - step, 1 - y)
        q_copy(source, sibling, 0).wait_recv()
        q_copy(source, sibling, 3 * depth + step).start()

    @pl.loop(0, n // 2)
    def _(step):
        q_copy(2 * step + 1 - core, sibling, 0).wait_recv()

    def part_copies(target, out, into, kind, slot, landing):
        return [
            pltpu.make_async_remote_copy(
                src_ref=source,
                dst_ref=destination,
                send_sem=p_send.at[kind, i, slot],
                recv_sem=p_recv.at[kind, i, landing],
                device_id={"ctx": target},
                device_id_type=MESH,
            )
            for i, (source, destination) in enumerate(zip(out, into))
        ]

    def at(refs, i):
        return [ref.at[i] for ref in refs]

    def to_core(chip):
        return part_copies(sibling, at(core_out, chip), at(core_got, chip), 0, chip, chip)

    def to_across(its_z):
        return part_copies(across, at(cross_out, its_z), at(cross_got, its_z), 1, its_z, its_z)

    def to_z(target, source):
        return part_copies(
            device(target, y, core), at(deep_out, target), at(deep_got, source), 2, target, source
        )

    def start(copies):
        for copy in copies:
            copy.start()

    def put(refs, i, partial):
        peak, total, weighted = partial
        row = lax.broadcasted_iota(jnp.int32, (8, rows), 0)
        refs[0][i] = weighted.astype(bf16)
        refs[1][i] = jnp.where(row == 0, peak, total)

    def get(refs, i):
        return refs[1][i, 0:1, :], refs[1][i, 1:2, :], refs[0][i].astype(f32)

    def merge(partials):
        peak = functools.reduce(jnp.maximum, [p for p, _, _ in partials])
        factors = [jnp.exp2(p - peak) for p, _, _ in partials]
        total = sum(f * t for f, (_, t, _) in zip(factors, partials))
        return peak, total, sum(f * w for f, (_, _, w) in zip(factors, partials))

    tile = chunk_of(context, 512)

    def exchange(i, step):
        rank = lax.rem(step, chips)
        its_z, its_y = place_at(rank)
        chip = its_z * 2 + its_y

        def mine():
            return mine_stat[i, 0:1, :], mine_stat[i, 1:2, :], mine_weighted[i]

        @pl.when((step < chips) if owners == 1 else (step >= 0))
        def _():
            put(core_out, chip, mine())
            start(to_core(chip))

        @pl.when((step >= chips) if owners == 1 else (step >= 0))
        def _():
            for copy in to_core(chip):
                copy.wait_recv()
            two = merge([mine(), get(core_got, chip)])

            @pl.when(rank < depth)
            def _():
                put(cross_out, its_z, two)
                start(to_across(its_z))

            @pl.when(rank >= depth)
            def _():
                for copy in to_across(its_z):
                    copy.wait_recv()
                put(deep_out, its_z, merge([two, get(cross_got, its_z)]))

                @pl.when(its_z != z)
                def _():
                    start(to_z(its_z, z))

    @pl.loop(0, kv_heads // 2)
    def _(pair):
        steps = [2 * pair, 2 * pair + 1]
        heads = [head_at(step) for step in steps]
        for step in steps:

            @pl.when(step + ahead < kv_heads)
            def _():
                load(step + ahead)

        @pl.when(pair == kv_heads // 4)
        def _():
            w_copy.start()

        empty = jnp.zeros((rows, head_dim), bf16)
        q0, q1 = [q_all[:, h].astype(f32).reshape(rows, head_dim).astype(bf16) for h in heads]
        q = jnp.concatenate(
            [jnp.concatenate([q0, empty], axis=1), jnp.concatenate([empty, q1], axis=1)], axis=0
        )
        for h in heads:
            k_copy(h).wait()
            v_copy(h).wait()
        partials = [[], []]
        for t in range(0, context, tile):
            span = pl.ds(t, tile)
            scores = lax.dot_general(
                jnp.concatenate([k_buf[h, span, :] for h in heads], axis=1),
                q,
                (((1,), (1,)), ((), ())),
                preferred_element_type=f32,
            )
            peak = jnp.max(scores, axis=0, keepdims=True) * scale
            exponent = jnp.exp2(scores * scale - peak)
            total = jnp.sum(exponent, axis=0, keepdims=True)
            weights = exponent.astype(bf16)
            for i, h in enumerate(heads):
                half = slice(i * rows, (i + 1) * rows)
                weighted = lax.dot_general(
                    v_buf[h, span, :],
                    weights[:, half],
                    (((0,), (0,)), ((), ())),
                    preferred_element_type=f32,
                )
                partials[i].append((peak[:, half], total[:, half], weighted))
        for i in range(2):
            peak, total, weighted = merge(partials[i])
            mine_weighted[i] = weighted
            mine_stat[i, 0:1, :] = peak
            mine_stat[i, 1:2, :] = total
        for i, step in enumerate(steps):
            exchange(i, step)

    deep_got[0][z] = deep_out[0][z]
    deep_got[1][z] = deep_out[1][z]

    @pl.loop(1, depth)
    def _(step):
        for copy in to_z(z, lax.rem(z + step, depth)):
            copy.wait_recv()

    _, total, weighted = merge([get(deep_got, i) for i in range(depth)])
    attended = (weighted / total).astype(bf16)

    unit = lax.broadcasted_iota(jnp.int32, (units, rows), 0)
    column = lax.broadcasted_iota(jnp.int32, (units, rows), 1)
    first = lax.rem(me, owners) * own_heads
    blocks = []
    for g in range(own_heads):
        place = (
            lax.div(unit, own_units) * own_rows + (first + g) * own_units + lax.rem(unit, own_units)
        )
        pick = jnp.where(column == place, 1.0, 0.0).astype(bf16)
        blocks.append(
            lax.dot_general(
                pick, attended, (((1,), (1,)), ((), ())), preferred_element_type=f32
            ).astype(bf16)
        )
    own_block = jnp.concatenate(blocks, axis=1) if own_heads > 1 else blocks[0]

    w_copy.wait()

    def core_copy(c):
        return pltpu.make_async_remote_copy(
            src_ref=y_out.at[c, 1 - core],
            dst_ref=core_in.at[c],
            send_sem=y_send.at[0, c],
            recv_sem=y_recv.at[0, c],
            device_id={"ctx": sibling},
            device_id_type=MESH,
        )

    def across_copy(c):
        return pltpu.make_async_remote_copy(
            src_ref=across_out.at[c],
            dst_ref=across_in.at[c],
            send_sem=y_send.at[1, c],
            recv_sem=y_recv.at[1, c],
            device_id={"ctx": across},
            device_id_type=MESH,
        )

    def z_copy(c, target, source):
        return pltpu.make_async_remote_copy(
            src_ref=z_out.at[c, target],
            dst_ref=z_in.at[c, source],
            send_sem=z_send.at[c, target],
            recv_sem=z_recv.at[c, source],
            device_id={"ctx": device(target, y, core)},
            device_id_type=MESH,
        )

    chunks = y_out.shape[0]
    cols = y_out.shape[-1]
    for c in range(chunks):
        product = jnp.dot(
            own_block, w_buf[:, c * cols : (c + 1) * cols], preferred_element_type=f32
        )
        for k in range(n):
            y_out[c, k % 2, k // 2 % 2, k // 4] = product[
                k * own_units : (k + 1) * own_units
            ].astype(bf16)
        core_copy(c).start()
    for c in range(chunks):
        core_copy(c).wait_recv()
        across_out[c] = (
            y_out[c, core, 1 - y].astype(f32) + core_in[c, 1 - y].astype(f32)
        ).astype(bf16)
        across_copy(c).start()
    for c in range(chunks):
        own_sum = y_out[c, core, y].astype(f32) + core_in[c, y].astype(f32)
        across_copy(c).wait_recv()
        z_out[c] = (own_sum + across_in[c].astype(f32)).astype(bf16)

        @pl.loop(1, depth)
        def _(step):
            z_copy(c, lax.rem(z + step, depth), z).start()

        z_in[c, z] = z_out[c, z]
    branches = []
    for c in range(chunks):

        @pl.loop(1, depth)
        def _(step):
            z_copy(c, z, lax.rem(z + step, depth)).wait_recv()

        branches.append(jnp.sum(z_in[c].astype(f32), axis=0))
    squares = sum(jnp.sum(b * b, axis=1, keepdims=True) for b in branches)
    inverse = lax.rsqrt(squares / width + 1e-06)
    for c, branch in enumerate(branches):
        span = pl.ds(c * cols, cols)
        gain = gain_ref[span].reshape(1, cols)
        out_ref[:, span] = res_ref[:, span].astype(f32) + branch * inverse * gain

    @pl.loop(0, n)
    def _(step):
        @pl.when(step != 2 * depth)
        def _():
            q_copy(me, sibling, step).wait_send()

    @pl.loop(0, chips)
    def _(chip):
        for copy in to_core(chip):
            copy.wait_send()

    @pl.loop(0, depth)
    def _(its_z):
        for copy in to_across(its_z):
            copy.wait_send()

        @pl.when(its_z != z)
        def _():
            for copy in to_z(its_z, z):
                copy.wait_send()

    for c in range(chunks):
        core_copy(c).wait_send()
        across_copy(c).wait_send()

        @pl.loop(1, depth)
        def _(step):
            z_copy(c, lax.rem(z + step, depth), z).wait_send()


def shards(n, queries, keys, values, residual, post_gain, out_weight):
    kv_heads, context, head_dim = keys.shape
    own_units, all_width = queries.shape
    head_count = all_width // head_dim
    group_size = head_count // kv_heads
    own_rows = own_units * group_size
    rows = n * own_rows
    width = residual.shape[1]
    cols = chunk_of(width, 2688)
    chunks = width // cols
    depth = n // 4
    vmem = pl.BlockSpec(memory_space=pltpu.VMEM)
    hbm = pl.BlockSpec(memory_space=pl.ANY)
    dma = pltpu.SemaphoreType.DMA

    def partials(count):
        return [
            pltpu.VMEM((count, head_dim, rows), bf16),
            pltpu.VMEM((count, 8, rows), f32),
        ]

    return pl.pallas_call(
        functools.partial(kernel, n, group_size),
        out_shape=jax.ShapeDtypeStruct((own_units, width), f32),
        in_specs=[vmem, hbm, hbm, vmem, vmem, hbm],
        out_specs=vmem,
        scratch_shapes=[
            pltpu.VMEM(keys.shape, bf16),
            pltpu.VMEM(values.shape, bf16),
            pltpu.VMEM(out_weight.shape, bf16),
            pltpu.VMEM((n, kv_heads, own_rows, head_dim), bf16),
            partials(n // 2),
            partials(n // 2),
            partials(depth),
            partials(depth),
            partials(depth),
            partials(depth),
            pltpu.VMEM((2, head_dim, rows), f32),
            pltpu.VMEM((2, 8, rows), f32),
            pltpu.VMEM((chunks, 2, 2, depth, own_units, cols), bf16),
            pltpu.VMEM((chunks, 2, depth, own_units, cols), bf16),
            pltpu.VMEM((chunks, depth, own_units, cols), bf16),
            pltpu.VMEM((chunks, depth, own_units, cols), bf16),
            pltpu.VMEM((chunks, depth, own_units, cols), bf16),
            pltpu.VMEM((chunks, depth, own_units, cols), bf16),
            dma((kv_heads,)),
            dma((kv_heads,)),
            dma,
            dma((n,)),
            dma((n,)),
            dma((3, 2, n // 2)),
            dma((3, 2, n // 2)),
            dma((2, chunks)),
            dma((2, chunks)),
            dma((chunks, depth)),
            dma((chunks, depth)),
        ],
        compiler_params=pltpu.CompilerParams(
            collective_id=0, has_side_effects=True, vmem_limit_bytes=56 * 2**20
        ),
        cost_estimate=pl.CostEstimate(
            flops=4 * kv_heads * context * rows * head_dim,
            bytes_accessed=4 * kv_heads * context * head_dim,
            transcendentals=kv_heads * context * rows,
        ),
    )(queries, keys, values, residual, post_gain, out_weight)


def solution(mesh):
    in_specs = (
        P(("groups", "ctx"), None),
        P(None, ("groups", "ctx"), None),
        P(None, ("groups", "ctx"), None),
        P(("groups", "ctx"), None),
        P(),
        P("ctx", None),
    )
    out_specs = P(("groups", "ctx"), None)
    return jax.shard_map(
        functools.partial(shards, mesh.shape["ctx"]),
        mesh=mesh,
        in_specs=in_specs,
        out_specs=out_specs,
        check_vma=False,
    )
```
